256 devices in a mesh: tm: 8 (over y_hi, x), space: 32 (over z, y_lo, core).
Axes of the slice: x: 4, y: 4 (y_hi: 2, y_lo: 2; y = y_hi * 2 + y_lo), z: 8, core: 2. Of those that a mesh axis runs over, the one named last changes fastest.
Arguments:
- initial: float32 [32, 131072], P(None, 'space'), may hold values from -6 to 6
- c_guess: float32 [8, 32, 131072], P('tm', None, 'space'), may hold values from -6 to 6
- forcing: float32 [64, 32, 131072], P('tm', None, 'space'), may hold values from -2 to 2
- fine_blocks: float32 [4, 16, 16], replicated, may hold values from -0.08 to 1.08, as said below
- coarse_blocks: float32 [4, 16, 16], replicated, may hold values from -0.08 to 1.08, as said below
Outputs:
- trajectory: float32 [64, 32, 131072], P('tm', None, 'space')
The draws below stay inside these ranges and needn't reach their ends.
Inputs may be any that keep to these rules, and one draw needn't show every extreme that they name: `fine_blocks`: each of the four matrices is a diagonal (decays below 1, or couplings of 0.8) plus small independent entries. `coarse_blocks`: as fine_blocks, with stronger decays.
All inputs are finite; a program needn't handle non-finite values.
Results may differ from the reference program's by a relative error of at most 0.0001.
Values sent between devices are 32-bit elements; how exact they have to be, the bound alone decides.
No kernel may reach another device: no remote copies, remote signals or barrier semaphores. Data moves between devices by JAX's collectives and lax.ppermute only.
A program may use at most 64 MiB of HBM per device.

```python
import math
import jax
import jax.numpy as jnp
from jax import lax

COND = 16
M = 8
SEG = 131072
COARSE = 8
STEPS = 64


def make_blocks(key, low_rate, high_rate):
    key_rates, key_noise = jax.random.split(key)
    decay_rates = jnp.exp(jax.random.uniform(key_rates, (2, COND), jnp.float32, math.log(low_rate), math.log(high_rate)))
    decays = jnp.exp(-decay_rates)
    noise = jnp.clip(jax.random.normal(key_noise, (4, COND, COND), jnp.float32), -4.0, 4.0) * 0.02
    identity = jnp.eye(COND, dtype=jnp.float32)
    diagonals = jnp.stack([decays[0], 0.8 * jnp.ones((COND,), jnp.float32), decays[1], 0.8 * jnp.ones((COND,), jnp.float32)])
    return diagonals[:, :, None] * identity[None] + noise


def draw_fine_blocks(key, part):
    key = jax.random.fold_in(key, 11)
    return make_blocks(key, 1.0 / 400.0, 1.0 / 25.0)


def draw_coarse_blocks(key, part):
    key = jax.random.fold_in(key, 23)
    return make_blocks(key, 8.0 / 400.0, 8.0 / 25.0)


def steps_of(stream_key, dims, cuts, low, largest):
    def one(axis_at, parts):
        draws = jax.random.uniform(jax.random.fold_in(jax.random.fold_in(stream_key, 6), axis_at), (parts,), jnp.float32, low / len(cuts), largest / len(cuts))
        return jnp.repeat(jnp.exp(draws), dims[axis_at] // parts).reshape((-1,) + (1,) * (len(dims) - axis_at - 1))

    factor_of = one(*cuts[0])
    for cut in cuts[1:]:
        factor_of = factor_of * one(*cut)
    return factor_of


def bell_draw(rng, shape, deviation, reach, shards=(), kind=jnp.bfloat16):
    array = jax.random.normal(rng, shape, jnp.float32) * deviation
    if len(shards) > 0:
        array = steps_of(rng, shape, shards, -0.22, 0.18) * array
    return jnp.clip(array, min=-reach, max=reach).astype(kind)


def setup_inputs(seed: int = 0) -> dict:
    arg_keys = jax.random.split(jax.random.key(seed), 6)
    return {
        "initial": bell_draw(arg_keys[0], (2 * COND, SEG), 1.0, 6.0, ((1, 32),), jnp.float32),
        "c_guess": bell_draw(arg_keys[1], (COARSE, 2 * COND, SEG), 1.0, 6.0, ((0, 8), (2, 32)), jnp.float32),
        "forcing": bell_draw(arg_keys[2], (STEPS, 2 * COND, SEG), 0.3, 2.0, ((0, 8), (2, 32)), jnp.float32),
        "fine_blocks": draw_fine_blocks(jax.random.fold_in(arg_keys[5], 71), 0),
        "coarse_blocks": draw_coarse_blocks(jax.random.fold_in(arg_keys[5], 71), 0),
    }


def mix(matrix, values):
    return jnp.einsum("ij,gjs->gis", matrix, values, precision=lax.Precision.HIGHEST)


def advance(state, blocks):
    conductors = blocks.shape[1]
    voltage = state[:, :conductors]
    current = state[:, conductors:]
    zero_col = jnp.zeros_like(current[:, :, :1])
    current_left = jnp.concatenate([zero_col, current[:, :, :-1]], axis=2)
    voltage_new = mix(blocks[0], voltage) - mix(blocks[1], current - current_left)
    voltage_right = jnp.concatenate([voltage_new[:, :, 1:], zero_col], axis=2)
    current_new = mix(blocks[2], current) - mix(blocks[3], voltage_right - voltage_new)
    return jnp.concatenate([voltage_new, current_new], axis=1)


def relax(starting, sources, blocks):
    state_now = starting
    kept_states = []
    for j in range(M - 1):
        state_now = advance(state_now, blocks) + sources[:, j]
        kept_states.append(state_now)
    return jnp.stack(kept_states, axis=1), state_now


def reference(initial, c_guess, forcing, fine_blocks, coarse_blocks):
    groups = c_guess.shape[0]
    sources = forcing.reshape(groups, M, forcing.shape[1], forcing.shape[2])
    starting = jnp.concatenate([initial[None], c_guess[:-1]], axis=0)
    f_first, final_state = relax(starting, sources, fine_blocks)
    c_value = advance(final_state, fine_blocks) + sources[:, M - 1]
    starting = jnp.concatenate([initial[None], c_value[:-1]], axis=0)
    f_second, final_state = relax(starting, sources, fine_blocks)
    resid = advance(final_state, fine_blocks) + sources[:, M - 1] - c_value
    correction = jnp.zeros_like(resid[:1])
    found = []
    for k in range(groups):
        correction = advance(correction, coarse_blocks) + resid[k:k + 1]
        found.append(correction[0])
    corrected = c_value + jnp.stack(found, axis=0)
    whole = jnp.concatenate([f_second, corrected[:, None]], axis=1)
    return whole.reshape(forcing.shape)
```

```python
import jax
import jax.numpy as jnp
from jax import lax
from jax.experimental import pallas as pl
from jax.experimental.pallas import tpu as pltpu
from jax.sharding import PartitionSpec as P

LANES = 128
REACH = 32
COND = 16
ROWS = 2 * COND
VMEM_LIMIT = 48 * 1024 * 1024


def iota(shape, axis):
    return lax.broadcasted_iota(jnp.int32, shape, axis)


def pack_edge(tile, base):
    lane = iota((8, LANES), 1)
    out = jnp.zeros((8, LANES), jnp.float32)
    for g in range(4):
        part = pltpu.roll(tile[8 * g : 8 * g + 8], (REACH * g - base) % LANES, 1)
        out = jnp.where(lane // REACH == g, part, out)
    return out


def unpack_edge(packed, base):
    return jnp.concatenate(
        [pltpu.roll(packed, (base - REACH * g) % LANES, 1) for g in range(4)], axis=0
    )


def halo_of_edges(from_left, from_right):
    lane = iota((ROWS, LANES), 1)
    right = jnp.where(lane < REACH, unpack_edge(from_right, 0), 0.0)
    return jnp.where(lane >= LANES - REACH, unpack_edge(from_left, LANES - REACH), right)


def pack_halo(halo):
    lane = iota((COND, LANES), 1)
    outer = (lane < REACH) | (lane >= LANES - REACH)
    return jnp.where(outer, halo[:COND], pltpu.roll(halo[COND:], LANES // 2, 1))


def unpack_halo(packed):
    return jnp.concatenate([packed, pltpu.roll(packed, LANES // 2, 1)], axis=0)


def join_halo(right, left):
    return jnp.where(iota((ROWS, LANES), 1) < LANES // 2, right, left)


def end_flags(index, size):
    at_left = jnp.where(index == 0, 1.0, 0.0).astype(jnp.float32)
    at_right = jnp.where(index == size - 1, 1.0, 0.0).astype(jnp.float32)
    return at_left, at_right


def fix_ends(last, halo, flags):
    at_left, at_right = flags
    lane = iota((ROWS, LANES), 1)
    row = iota((ROWS, LANES), 0)
    keep = 1.0 - jnp.where(lane < LANES // 2, at_right, at_left)
    ghost = jnp.where((lane == 0) & (row >= COND), at_right, 0.0)
    return halo * keep + pltpu.roll(last, 1, 1) * ghost


def step(state, weights, width, flags):
    columns = state.shape[1]
    pieces = []
    for b in range(0, columns, width):
        e = b + width
        pieces.append(state[:, b : e - LANES])
        pieces.append(fix_ends(state[:, e - 2 * LANES : e - LANES], state[:, e - LANES : e], flags))
    state = jnp.concatenate(pieces, axis=1)
    high = state.astype(jnp.bfloat16)
    low = (state - high.astype(jnp.float32)).astype(jnp.bfloat16)
    product = jnp.dot(
        weights,
        jnp.concatenate([high, high, low, high], axis=0),
        preferred_element_type=jnp.float32,
    )
    outs = []
    for b in range(0, columns, width):
        e = b + width
        here = product[:ROWS, b:e]
        from_left = pltpu.roll(product[ROWS : 2 * ROWS, b:e], 1, 1)
        from_right = pltpu.roll(product[2 * ROWS :, b:e], width - 1, 1)
        outs.append(
            jnp.concatenate(
                [here[:COND] + from_left[:COND], here[COND:] + from_left[COND:] + from_right], axis=0
            )
        )
    return outs[0] if len(outs) == 1 else jnp.concatenate(outs, axis=1)


def weights_kernel(blocks_ref, out_ref):
    p_v, k_v, p_i, k_i = (blocks_ref[m] for m in range(4))

    def product(a, b):
        return jnp.dot(
            a, b, precision=lax.Precision.HIGHEST, preferred_element_type=jnp.float32
        )

    kp = product(k_i, p_v)
    kk = product(k_i, k_v)
    zero = jnp.zeros_like(kk)
    rows = [[p_v, -k_v], [kp, p_i - 2.0 * kk], [zero, k_v], [zero, kk], [-kp, kk]]
    whole = jnp.concatenate([jnp.concatenate(r, axis=1) for r in rows], axis=0)
    high = whole.astype(jnp.bfloat16)
    rest = whole - high.astype(jnp.float32)
    low = rest.astype(jnp.bfloat16)
    least = (rest - low.astype(jnp.float32)).astype(jnp.bfloat16)
    out_ref[...] = jnp.concatenate([high, low, high, least], axis=1)


def make_weights(blocks):
    return pl.pallas_call(
        weights_kernel,
        out_shape=jax.ShapeDtypeStruct((5 * COND, 4 * ROWS), jnp.bfloat16),
        name="weights",
    )(blocks)


def edges_kernel(f_first, f_last, c_first, c_last, i_first, i_last, low_ref, high_ref):
    count = f_first.shape[0]
    for n in range(count):
        low_ref[n] = pack_edge(f_first[n], 0)
        high_ref[n] = pack_edge(f_last[n], LANES - REACH)
    low_ref[count] = pack_edge(c_first[0], 0)
    high_ref[count] = pack_edge(c_last[0], LANES - REACH)
    low_ref[count + 1] = pack_edge(i_first[...], 0)
    high_ref[count + 1] = pack_edge(i_last[...], LANES - REACH)


def cut_edges(forcing, c_guess, initial):
    count, _, length = forcing.shape
    end = length // LANES - 1

    def both(shape, at):
        return [pl.BlockSpec(shape, lambda g, a=a: at(a)) for a in (0, end)]

    shape = jax.ShapeDtypeStruct((count + 2, 8, LANES), jnp.float32)
    whole = pl.BlockSpec(shape.shape, lambda g: (0, 0, 0))
    return pl.pallas_call(
        edges_kernel,
        grid=(1,),
        out_shape=(shape, shape),
        in_specs=both((count, ROWS, LANES), lambda a: (0, 0, a))
        + both((1, ROWS, LANES), lambda a: (0, 0, a))
        + both((ROWS, LANES), lambda a: (0, a)),
        out_specs=(whole, whole),
        name="edges",
    )(forcing, forcing, c_guess, c_guess, initial, initial)


def write_parts(out_ref, main, halo, at):
    groups = out_ref.shape[0]
    length = main.shape[1]
    part = length // groups
    tiles = part // LANES

    def tile(k):
        if k < 0 or k == length // LANES:
            return halo
        return main[:, k * LANES : (k + 1) * LANES]

    for j in range(groups):
        for i in range(tiles):
            out_ref[j, at + ROWS * i : at + ROWS * (i + 1), :] = tile(j * tiles + i)
        rim = join_halo(tile((j + 1) * tiles), tile(j * tiles - 1))
        out_ref[j, at + ROWS * tiles : at + ROWS * tiles + COND, :] = pack_halo(rim)


def source_kernel(
    forcing_ref, guess_ref, initial_ref, left_ref, right_ref, weights_ref, out_ref, own_ref, state_ref
):
    n = pl.program_id(0)
    count = pl.num_programs(0)
    length = forcing_ref.shape[2]
    groups = out_ref.shape[0]
    part = length // groups
    tiles = part // LANES
    flags = end_flags(lax.axis_index("space"), lax.axis_size("space"))

    @pl.when(n == 0)
    def _():
        state_ref[...] = jnp.zeros_like(state_ref)

    state = step(state_ref[...], weights_ref[...], length + LANES, flags)
    main = state[:, :length] + forcing_ref[0]
    halo = state[:, length:] + halo_of_edges(left_ref[n], right_ref[n])
    state_ref[:, :length] = main
    state_ref[:, length:] = halo

    @pl.when(n == count - 1)
    def _():
        guess_halo = halo_of_edges(left_ref[count], right_ref[count])
        write_parts(out_ref, guess_ref[0], guess_halo, 0)
        write_parts(out_ref, state_ref[:, :length], state_ref[:, length:], tiles * ROWS + COND)
        j = lax.axis_index("tm")
        last = length // LANES - 1
        halo = halo_of_edges(left_ref[count + 1], right_ref[count + 1])

        def tile(k):
            inside = initial_ref[
                :, pl.ds(pl.multiple_of(jnp.clip(k, 0, last) * LANES, LANES), LANES)
            ]
            outside = jnp.where((k < 0) | (k > last), 1.0, 0.0).astype(jnp.float32)
            return inside * (1.0 - outside) + halo * outside

        own_ref[:, :part] = initial_ref[:, pl.ds(pl.multiple_of(j * part, LANES), part)]
        own_ref[:, part:] = join_halo(tile((j + 1) * tiles), tile(j * tiles - 1))


def source_chain(forcing, c_guess, initial, left, right, weights, groups):
    count, _, length = forcing.shape
    part = length // groups
    rows = 2 * (part // LANES * ROWS + COND)
    return pl.pallas_call(
        source_kernel,
        grid=(count,),
        out_shape=(
            jax.ShapeDtypeStruct((groups, rows, LANES), jnp.float32),
            jax.ShapeDtypeStruct((ROWS, part + LANES), jnp.float32),
        ),
        in_specs=[
            pl.BlockSpec((1, ROWS, length), lambda n: (n, 0, 0)),
            pl.BlockSpec((1, ROWS, length), lambda n: (0, 0, 0)),
            pl.BlockSpec((ROWS, length), lambda n: (0, 0)),
            pl.BlockSpec(left.shape, lambda n: (0, 0, 0)),
            pl.BlockSpec(right.shape, lambda n: (0, 0, 0)),
            pl.BlockSpec(weights.shape, lambda n: (0, 0)),
        ],
        out_specs=(
            pl.BlockSpec((groups, rows, LANES), lambda n: (0, 0, 0)),
            pl.BlockSpec((ROWS, part + LANES), lambda n: (0, 0)),
        ),
        scratch_shapes=[pltpu.VMEM((ROWS, length + LANES), jnp.float32)],
        compiler_params=pltpu.CompilerParams(vmem_limit_bytes=VMEM_LIMIT),
        name="source_chain",
    )(forcing, c_guess, initial, left, right, weights)


def coarse_kernel(parts_ref, own_ref, fine_ref, coarse_ref, out_ref, state_ref, value_ref):
    groups = parts_ref.shape[0]
    width = own_ref.shape[1]
    part = width - LANES
    tiles = part // LANES
    size = tiles * ROWS + COND
    space, spaces = lax.axis_index("space"), lax.axis_size("space")
    flags = end_flags(space * groups + lax.axis_index("tm"), spaces * groups)

    def ring(t, at):
        pieces = [parts_ref[t, at + ROWS * i : at + ROWS * (i + 1), :] for i in range(tiles)]
        pieces.append(unpack_halo(parts_ref[t, at + ROWS * tiles : at + size, :]))
        return jnp.concatenate(pieces, axis=1)

    def put(t, at, ring, rim):
        for i in range(tiles):
            out_ref[t, at + ROWS * i : at + ROWS * (i + 1), :] = ring[:, i * LANES : (i + 1) * LANES]
        if rim:
            out_ref[t, at + ROWS * tiles : at + size, :] = pack_halo(ring[:, part:])

    def cols(t):
        return slice(t * width, (t + 1) * width)

    def relax(columns):
        def one(i, carry):
            state_ref[:, :columns] = step(state_ref[:, :columns], fine_ref[...], width, flags)
            return carry

        lax.fori_loop(0, 8, one, 0)

    state_ref[:, cols(0)] = own_ref[...]
    for t in range(1, groups):
        state_ref[:, cols(t)] = ring(t - 1, 0)
    relax(groups * width)
    for t in range(groups):
        value_ref[:, cols(t)] = state_ref[:, cols(t)] + ring(t, size)

    for t in range(groups - 1):
        state_ref[:, cols(t)] = value_ref[:, cols(t)] - ring(t, 0)
    relax((groups - 1) * width)

    put(0, 0, own_ref[...], True)
    put(0, size, value_ref[:, cols(0)], False)
    correction = None
    for t in range(1, groups):
        resid = state_ref[:, cols(t - 1)]
        if correction is None:
            correction = resid
        else:
            correction = step(correction, coarse_ref[...], width, flags) + resid
        put(t, 0, value_ref[:, cols(t - 1)], True)
        put(t, size, value_ref[:, cols(t)] + correction, False)


def coarse_solve(parts, own, fine, coarse):
    groups, rows, _ = parts.shape
    width = own.shape[1]
    return pl.pallas_call(
        coarse_kernel,
        out_shape=jax.ShapeDtypeStruct((groups, rows - COND, LANES), jnp.float32),
        scratch_shapes=[
            pltpu.VMEM((ROWS, groups * width), jnp.float32),
            pltpu.VMEM((ROWS, groups * width), jnp.float32),
        ],
        compiler_params=pltpu.CompilerParams(vmem_limit_bytes=VMEM_LIMIT),
        name="coarse_solve",
    )(parts, own, fine, coarse)


def final_kernel(forcing_ref, parts_ref, left_ref, right_ref, weights_ref, out_ref, state_ref):
    n = pl.program_id(0)
    count = pl.num_programs(0)
    length = forcing_ref.shape[2]
    groups = parts_ref.shape[0]
    tiles = length // groups // LANES
    size = tiles * ROWS + COND
    flags = end_flags(lax.axis_index("space"), lax.axis_size("space"))

    def main(at):
        return jnp.concatenate(
            [
                parts_ref[j, at + ROWS * i : at + ROWS * (i + 1), :]
                for j in range(groups)
                for i in range(tiles)
            ],
            axis=1,
        )

    @pl.when(n == 0)
    def _():
        state_ref[:, :length] = main(0)
        state_ref[:, length:] = join_halo(
            unpack_halo(parts_ref[groups - 1, ROWS * tiles : size, :]),
            unpack_halo(parts_ref[0, ROWS * tiles : size, :]),
        )

    @pl.when(n < count - 1)
    def _():
        state = step(state_ref[...], weights_ref[...], length + LANES, flags)
        main = state[:, :length] + forcing_ref[0]
        state_ref[:, :length] = main
        state_ref[:, length:] = state[:, length:] + halo_of_edges(left_ref[n], right_ref[n])
        out_ref[0] = main

    @pl.when(n == count - 1)
    def _():
        out_ref[0] = main(size)


def final_chain(forcing, parts, left, right, weights):
    count, _, length = forcing.shape
    return pl.pallas_call(
        final_kernel,
        grid=(count,),
        out_shape=jax.ShapeDtypeStruct(forcing.shape, jnp.float32),
        in_specs=[
            pl.BlockSpec((1, ROWS, length), lambda n: (jnp.minimum(n, count - 2), 0, 0)),
            pl.BlockSpec(parts.shape, lambda n: (0, 0, 0)),
            pl.BlockSpec(left.shape, lambda n: (0, 0, 0)),
            pl.BlockSpec(right.shape, lambda n: (0, 0, 0)),
            pl.BlockSpec(weights.shape, lambda n: (0, 0)),
        ],
        out_specs=pl.BlockSpec((1, ROWS, length), lambda n: (n, 0, 0)),
        scratch_shapes=[pltpu.VMEM((ROWS, length + LANES), jnp.float32)],
        compiler_params=pltpu.CompilerParams(vmem_limit_bytes=VMEM_LIMIT),
        name="final_chain",
    )(forcing, parts, left, right, weights)


def body(initial, c_guess, forcing, fine_blocks, coarse_blocks):
    groups = lax.axis_size("tm")
    spaces = lax.axis_size("space")
    low, high = cut_edges(forcing, c_guess, initial)
    right = lax.ppermute(low, "space", [(i, (i - 1) % spaces) for i in range(spaces)])
    left = lax.ppermute(high, "space", [(i, (i + 1) % spaces) for i in range(spaces)])
    fine = make_weights(fine_blocks)
    coarse = make_weights(coarse_blocks)
    parts, own = source_chain(forcing, c_guess, initial, left, right, fine, groups)
    parts = lax.all_to_all(parts, "tm", 0, 0, tiled=True)
    parts = coarse_solve(parts, own, fine, coarse)
    parts = lax.all_to_all(parts, "tm", 0, 0, tiled=True)
    return final_chain(forcing, parts, left, right, fine)


def solution(mesh):
    in_specs = (P(None, "space"), P("tm", None, "space"), P("tm", None, "space"), P(), P())
    out_specs = P("tm", None, "space")
    return jax.shard_map(body, mesh=mesh, in_specs=in_specs, out_specs=out_specs, check_vma=False)
```

```python
import jax
import jax.numpy as jnp
from jax import lax
from jax.experimental import pallas as pl
from jax.experimental.pallas import tpu as pltpu
from jax.sharding import PartitionSpec as P

LANES = 128
REACH = 32
COND = 16
ROWS = 2 * COND
VMEM_LIMIT = 20 * 1024 * 1024


def iota(shape, axis):
    return lax.broadcasted_iota(jnp.int32, shape, axis)


def pack_edge(tile, base):
    lane = iota((8, LANES), 1)
    out = jnp.zeros((8, LANES), jnp.float32)
    for g in range(4):
        part = pltpu.roll(tile[8 * g : 8 * g + 8], (REACH * g - base) % LANES, 1)
        out = jnp.where(lane // REACH == g, part, out)
    return out


def unpack_edge(packed, base):
    return jnp.concatenate(
        [pltpu.roll(packed, (base - REACH * g) % LANES, 1) for g in range(4)], axis=0
    )


def halo_of_edges(from_left, from_right):
    lane = iota((ROWS, LANES), 1)
    right = jnp.where(lane < REACH, unpack_edge(from_right, 0), 0.0)
    return jnp.where(lane >= LANES - REACH, unpack_edge(from_left, LANES - REACH), right)


def pack_halo(halo):
    lane = iota((COND, LANES), 1)
    outer = (lane < REACH) | (lane >= LANES - REACH)
    return jnp.where(outer, halo[:COND], pltpu.roll(halo[COND:], LANES // 2, 1))


def unpack_halo(packed):
    return jnp.concatenate([packed, pltpu.roll(packed, LANES // 2, 1)], axis=0)


def join_halo(right, left):
    return jnp.where(iota((ROWS, LANES), 1) < LANES // 2, right, left)


def end_flags(index, size):
    at_left = jnp.where(index == 0, 1.0, 0.0).astype(jnp.float32)
    at_right = jnp.where(index == size - 1, 1.0, 0.0).astype(jnp.float32)
    return at_left, at_right


def fix_ends(last, halo, flags):
    at_left, at_right = flags
    lane = iota((ROWS, LANES), 1)
    row = iota((ROWS, LANES), 0)
    keep = 1.0 - jnp.where(lane < LANES // 2, at_right, at_left)
    ghost = jnp.where((lane == 0) & (row >= COND), at_right, 0.0)
    return halo * keep + pltpu.roll(last, 1, 1) * ghost


def step(state, weights, width, flags):
    columns = state.shape[1]
    pieces = []
    for b in range(0, columns, width):
        e = b + width
        pieces.append(state[:, b : e - LANES])
        pieces.append(fix_ends(state[:, e - 2 * LANES : e - LANES], state[:, e - LANES : e], flags))
    state = jnp.concatenate(pieces, axis=1)
    high = state.astype(jnp.bfloat16)
    low = (state - high.astype(jnp.float32)).astype(jnp.bfloat16)
    product = jnp.dot(
        weights,
        jnp.concatenate([high, high, low, high], axis=0),
        preferred_element_type=jnp.float32,
    )
    outs = []
    for b in range(0, columns, width):
        e = b + width
        here = product[:ROWS, b:e]
        from_left = pltpu.roll(product[ROWS : 2 * ROWS, b:e], 1, 1)
        from_right = pltpu.roll(product[2 * ROWS :, b:e], width - 1, 1)
        outs.append(
            jnp.concatenate(
                [here[:COND] + from_left[:COND], here[COND:] + from_left[COND:] + from_right], axis=0
            )
        )
    return outs[0] if len(outs) == 1 else jnp.concatenate(outs, axis=1)


def prepare_kernel(fine_ref, coarse_ref, forcing_ref, out_ref, staged_ref, sem):
    copy = pltpu.make_async_copy(forcing_ref, staged_ref, sem)
    copy.start()

    def product(a, b):
        return jnp.dot(
            a, b, precision=lax.Precision.HIGHEST, preferred_element_type=jnp.float32
        )

    for m, blocks_ref in enumerate((fine_ref, coarse_ref)):
        p_v, k_v, p_i, k_i = (blocks_ref[r] for r in range(4))
        kp = product(k_i, p_v)
        kk = product(k_i, k_v)
        zero = jnp.zeros_like(kk)
        rows = [[p_v, -k_v], [kp, p_i - 2.0 * kk], [zero, k_v], [zero, kk], [-kp, kk]]
        whole = jnp.concatenate([jnp.concatenate(r, axis=1) for r in rows], axis=0)
        high = whole.astype(jnp.bfloat16)
        rest = whole - high.astype(jnp.float32)
        low = rest.astype(jnp.bfloat16)
        least = (rest - low.astype(jnp.float32)).astype(jnp.bfloat16)
        out_ref[m] = jnp.concatenate([high, low, high, least], axis=1)
    copy.wait()


def prepare(fine_blocks, coarse_blocks, forcing):
    vmem = pl.BlockSpec(memory_space=pltpu.VMEM)
    return pl.pallas_call(
        prepare_kernel,
        out_shape=(
            pltpu.VMEM((2, 5 * COND, 4 * ROWS), jnp.bfloat16),
            pltpu.VMEM(forcing.shape, jnp.float32),
        ),
        in_specs=[vmem, vmem, pl.BlockSpec(memory_space=pltpu.HBM)],
        out_specs=(vmem, vmem),
        scratch_shapes=[pltpu.SemaphoreType.DMA],
        compiler_params=pltpu.CompilerParams(vmem_limit_bytes=VMEM_LIMIT),
        name="prepare",
    )(fine_blocks, coarse_blocks, pltpu.with_memory_space_constraint(forcing, pltpu.HBM))


def edges_kernel(
    f_first, f_last, c_first, c_last, i_first, i_last, low_ref, high_ref, low_guess_ref, high_guess_ref
):
    count = f_first.shape[0]
    for n in range(count):
        low_ref[n] = pack_edge(f_first[n], 0)
        high_ref[n] = pack_edge(f_last[n], LANES - REACH)
    low_guess_ref[...] = pack_edge(c_first[0], 0)
    high_guess_ref[...] = pack_edge(c_last[0], LANES - REACH)
    low_ref[count] = low_guess_ref[...]
    high_ref[count] = high_guess_ref[...]
    low_ref[count + 1] = pack_edge(i_first[...], 0)
    high_ref[count + 1] = pack_edge(i_last[...], LANES - REACH)


def cut_edges(forcing, c_guess, initial):
    count, _, length = forcing.shape
    end = length // LANES - 1

    def both(shape, at):
        return [pl.BlockSpec(shape, lambda g, a=a: at(a)) for a in (0, end)]

    shape = jax.ShapeDtypeStruct((count + 2, 8, LANES), jnp.float32)
    whole = pl.BlockSpec(shape.shape, lambda g: (0, 0, 0))
    guess = jax.ShapeDtypeStruct((8, LANES), jnp.float32)
    whole_guess = pl.BlockSpec(guess.shape, lambda g: (0, 0))
    return pl.pallas_call(
        edges_kernel,
        grid=(1,),
        out_shape=(shape, shape, guess, guess),
        in_specs=both((count, ROWS, LANES), lambda a: (0, 0, a))
        + both((1, ROWS, LANES), lambda a: (0, 0, a))
        + both((ROWS, LANES), lambda a: (0, a)),
        out_specs=(whole, whole, whole_guess, whole_guess),
        name="edges",
    )(forcing, forcing, c_guess, c_guess, initial, initial)


def write_parts(out_ref, main, halo, at):
    groups = out_ref.shape[0]
    length = main.shape[1]
    part = length // groups
    tiles = part // LANES

    def tile(k):
        if k < 0 or k == length // LANES:
            return halo
        return main[:, k * LANES : (k + 1) * LANES]

    for j in range(groups):
        for i in range(tiles):
            out_ref[j, at + ROWS * i : at + ROWS * (i + 1), :] = tile(j * tiles + i)
        rim = join_halo(tile((j + 1) * tiles), tile(j * tiles - 1))
        out_ref[j, at + ROWS * tiles : at + ROWS * tiles + COND, :] = pack_halo(rim)


def start_chain(main_ref, halo_ref, begin_ref, initial_ref, left_ref, right_ref, sem):
    is_first = lax.axis_index("tm") == 0
    last = left_ref.shape[0] - 1

    @pl.when(is_first)
    def _():
        pltpu.make_async_copy(initial_ref, main_ref, sem).start()
        halo_ref[...] = halo_of_edges(left_ref[last], right_ref[last])

    @pl.when(jnp.logical_not(is_first))
    def _():
        pltpu.make_async_copy(begin_ref, main_ref, sem).start()

    return pltpu.make_async_copy(begin_ref, main_ref, sem)


def advance(main, halo, source, left, right, weights, flags):
    length = main.shape[1]
    state = step(jnp.concatenate([main, halo], axis=1), weights, length + LANES, flags)
    return state[:, :length] + source, state[:, length:] + halo_of_edges(left, right)


def first_kernel(
    forcing_ref,
    begin_ref,
    initial_ref,
    guess_ref,
    left_ref,
    right_ref,
    begin_left_ref,
    begin_right_ref,
    weights_ref,
    out_ref,
    value_ref,
    own_ref,
    sems,
):
    count = forcing_ref.shape[0]
    length = forcing_ref.shape[2]
    flags = end_flags(lax.axis_index("space"), lax.axis_size("space"))
    main_ref, halo_ref = value_ref.at[:, :length], value_ref.at[:, length:]

    halo_ref[...] = halo_of_edges(begin_left_ref[...], begin_right_ref[...])
    begun = start_chain(
        main_ref, halo_ref, begin_ref, initial_ref, left_ref, right_ref, sems.at[0]
    )
    own = pltpu.make_async_copy(guess_ref.at[0], own_ref, sems.at[1])
    own.start()
    begun.wait()

    def one(n, carry):
        main, halo = advance(
            main_ref[...],
            halo_ref[...],
            forcing_ref[n],
            left_ref[n],
            right_ref[n],
            weights_ref[0],
            flags,
        )
        main_ref[...] = main
        halo_ref[...] = halo
        return carry

    lax.fori_loop(0, count, one, 0)
    own.wait()
    guess_halo = halo_of_edges(left_ref[count], right_ref[count])
    write_parts(out_ref, main_ref[...] - own_ref[...], halo_ref[...] - guess_halo, 0)


def first_chain(
    forcing, begin, initial, c_guess, left, right, begin_left, begin_right, weights, groups
):
    count, _, length = forcing.shape
    rows = length // groups // LANES * ROWS + COND
    anywhere = pl.BlockSpec(memory_space=pl.ANY)
    vmem = pl.BlockSpec(memory_space=pltpu.VMEM)
    return pl.pallas_call(
        first_kernel,
        out_shape=(
            jax.ShapeDtypeStruct((groups, rows, LANES), jnp.float32),
            jax.ShapeDtypeStruct((ROWS, length + LANES), jnp.float32),
        ),
        in_specs=[vmem, anywhere, anywhere, anywhere, vmem, vmem, vmem, vmem, vmem],
        out_specs=(vmem, vmem),
        scratch_shapes=[
            pltpu.VMEM((ROWS, length), jnp.float32),
            pltpu.SemaphoreType.DMA((2,)),
        ],
        compiler_params=pltpu.CompilerParams(vmem_limit_bytes=VMEM_LIMIT),
        cost_estimate=cost(count, length, forcing.size),
        name="first_chain",
    )(forcing, begin, initial, c_guess, left, right, begin_left, begin_right, weights)


def cost(steps, columns, elements):
    return pl.CostEstimate(
        flops=steps * columns * 80 * 128 * 16, bytes_accessed=8 * elements, transcendentals=0
    )


def coarse_kernel(parts_ref, weights_ref, out_ref, state_ref):
    groups = parts_ref.shape[0]
    tiles = (parts_ref.shape[1] - COND) // ROWS
    part = tiles * LANES
    width = part + LANES
    space, spaces = lax.axis_index("space"), lax.axis_size("space")
    flags = end_flags(space * groups + lax.axis_index("tm"), spaces * groups)

    def cols(t):
        return slice(t * width, (t + 1) * width)

    for t in range(groups - 1):
        for i in range(tiles):
            at = t * width + i * LANES
            state_ref[:, at : at + LANES] = parts_ref[t, ROWS * i : ROWS * (i + 1), :]
        state_ref[:, t * width + part : (t + 1) * width] = unpack_halo(
            parts_ref[t, ROWS * tiles : ROWS * tiles + COND, :]
        )

    def one(i, carry):
        state_ref[...] = step(state_ref[...], weights_ref[0], width, flags)
        return carry

    lax.fori_loop(0, 8, one, 0)

    out_ref[0] = jnp.zeros_like(out_ref[0])
    correction = None
    for t in range(1, groups):
        resid = state_ref[:, cols(t - 1)]
        if correction is None:
            correction = resid
        else:
            correction = step(correction, weights_ref[1], width, flags) + resid
        for i in range(tiles):
            out_ref[t, ROWS * i : ROWS * (i + 1), :] = correction[:, i * LANES : (i + 1) * LANES]


def coarse_solve(parts, weights):
    groups, rows, _ = parts.shape
    tiles = (rows - COND) // ROWS
    return pl.pallas_call(
        coarse_kernel,
        out_shape=jax.ShapeDtypeStruct((groups, ROWS * tiles, LANES), jnp.float32),
        scratch_shapes=[pltpu.VMEM((ROWS, (groups - 1) * (tiles + 1) * LANES), jnp.float32)],
        compiler_params=pltpu.CompilerParams(vmem_limit_bytes=VMEM_LIMIT),
        cost_estimate=cost(12, groups * tiles * LANES, parts.size),
        name="coarse_solve",
    )(parts, weights)


def second_kernel(
    forcing_ref,
    begin_ref,
    initial_ref,
    left_ref,
    right_ref,
    weights_ref,
    out_ref,
    states_ref,
    halo_ref,
    sems,
    out_sems,
):
    steps = out_sems.shape[0]
    length = forcing_ref.shape[2]
    flags = end_flags(lax.axis_index("space"), lax.axis_size("space"))

    halo = pltpu.make_async_copy(begin_ref.at[:, length:], halo_ref, sems.at[1])
    halo.start()
    halo.wait()
    begun = start_chain(
        states_ref.at[0],
        halo_ref,
        begin_ref.at[:, :length],
        initial_ref,
        left_ref,
        right_ref,
        sems.at[0],
    )

    def result(n):
        return pltpu.make_async_copy(states_ref.at[n + 1], out_ref.at[n], out_sems.at[n])

    begun.wait()

    def one(n, carry):
        main, halo = advance(
            states_ref[n],
            halo_ref[...],
            forcing_ref[n],
            left_ref[n],
            right_ref[n],
            weights_ref[0],
            flags,
        )
        states_ref[n + 1] = main
        halo_ref[...] = halo
        result(n).start()
        return carry

    lax.fori_loop(0, steps, one, 0)
    for n in range(steps):
        result(n).wait()


def second_chain(forcing, begin, initial, left, right, weights):
    count, _, length = forcing.shape
    hbm = pl.BlockSpec(memory_space=pltpu.HBM)
    anywhere = pl.BlockSpec(memory_space=pl.ANY)
    vmem = pl.BlockSpec(memory_space=pltpu.VMEM)
    return pl.pallas_call(
        second_kernel,
        out_shape=jax.ShapeDtypeStruct(forcing.shape, jnp.float32),
        in_specs=[vmem, anywhere, anywhere, vmem, vmem, vmem],
        out_specs=hbm,
        scratch_shapes=[
            pltpu.VMEM(forcing.shape, jnp.float32),
            pltpu.VMEM((ROWS, LANES), jnp.float32),
            pltpu.SemaphoreType.DMA((2,)),
            pltpu.SemaphoreType.DMA((count - 1,)),
        ],
        compiler_params=pltpu.CompilerParams(vmem_limit_bytes=VMEM_LIMIT),
        cost_estimate=cost(count, length, 2 * forcing.size),
        name="second_chain",
    )(forcing, begin, initial, left, right, weights)


def correct_kernel(value_ref, parts_ref, states_ref, out_ref):
    del states_ref
    groups = parts_ref.shape[0]
    tiles = out_ref.shape[2] // groups // LANES
    for j in range(groups):
        for i in range(tiles):
            at = (j * tiles + i) * LANES
            out_ref[0, :, at : at + LANES] = (
                value_ref[:, at : at + LANES] + parts_ref[j, ROWS * i : ROWS * (i + 1), :]
            )


def correct_last(value, parts, states):
    count, _, length = states.shape
    return pl.pallas_call(
        correct_kernel,
        grid=(1,),
        out_shape=jax.ShapeDtypeStruct(states.shape, jnp.float32),
        in_specs=[
            pl.BlockSpec(value.shape, lambda g: (0, 0)),
            pl.BlockSpec(parts.shape, lambda g: (0, 0, 0)),
            pl.BlockSpec(memory_space=pl.ANY),
        ],
        out_specs=pl.BlockSpec((1, ROWS, length), lambda g: (count - 1, 0, 0)),
        input_output_aliases={2: 0},
        compiler_params=pltpu.CompilerParams(vmem_limit_bytes=VMEM_LIMIT),
        name="correct_last",
    )(value, parts, states)


def body(initial, c_guess, forcing, fine_blocks, coarse_blocks):
    groups = lax.axis_size("tm")
    spaces = lax.axis_size("space")
    up = [(i, (i + 1) % spaces) for i in range(spaces)]
    down = [(b, a) for a, b in up]
    to_next = [(i, (i + 1) % groups) for i in range(groups)]

    def to_next_and(pairs):
        return [(t * spaces + a, u * spaces + b) for t, u in to_next for a, b in pairs]

    begin = lax.ppermute(c_guess[0], "tm", to_next)
    low, high, low_guess, high_guess = cut_edges(forcing, c_guess, initial)
    right = lax.ppermute(low, "space", down)
    left = lax.ppermute(high, "space", up)
    begin_right = lax.ppermute(low_guess, ("tm", "space"), to_next_and(down))
    begin_left = lax.ppermute(high_guess, ("tm", "space"), to_next_and(up))
    weights, staged = prepare(fine_blocks, coarse_blocks, forcing)
    parts, value = first_chain(
        staged, begin, initial, c_guess, left, right, begin_left, begin_right, weights, groups
    )
    parts = lax.all_to_all(parts, "tm", 0, 0, tiled=True)
    begin = lax.ppermute(value, "tm", to_next)
    parts = coarse_solve(parts, weights)
    parts = lax.all_to_all(parts, "tm", 0, 0, tiled=True)
    states = second_chain(staged, begin, initial, left, right, weights)
    return correct_last(value, parts, states)


def solution(mesh):
    in_specs = (P(None, "space"), P("tm", None, "space"), P("tm", None, "space"), P(), P())
    out_specs = P("tm", None, "space")
    return jax.shard_map(body, mesh=mesh, in_specs=in_specs, out_specs=out_specs, check_vma=False)
```

```python
import jax
import jax.numpy as jnp
from jax import lax
from jax.experimental import pallas as pl
from jax.experimental.pallas import tpu as pltpu
from jax.sharding import PartitionSpec as P

LANES = 128
REACH = 32
COND = 16
ROWS = 2 * COND
ONCE = 5 * COND
TWICE = 9 * COND
FINE, COARSE, COARSE_TWICE, OPERATORS = 0, ONCE, 2 * ONCE, 2 * ONCE + TWICE
VMEM_LIMIT = 20 * 1024 * 1024


def iota(shape, axis):
    return lax.broadcasted_iota(jnp.int32, shape, axis)


def pack_edge(tile, base):
    lane = iota((8, LANES), 1)
    out = jnp.zeros((8, LANES), jnp.float32)
    for g in range(4):
        part = pltpu.roll(tile[8 * g : 8 * g + 8], (REACH * g - base) % LANES, 1)
        out = jnp.where(lane // REACH == g, part, out)
    return out


def unpack_edge(packed, base):
    return jnp.concatenate(
        [pltpu.roll(packed, (base - REACH * g) % LANES, 1) for g in range(4)], axis=0
    )


def halo_of_edges(from_left, from_right):
    lane = iota((ROWS, LANES), 1)
    right = jnp.where(lane < REACH, unpack_edge(from_right, 0), 0.0)
    return jnp.where(lane >= LANES - REACH, unpack_edge(from_left, LANES - REACH), right)


def pack_halo(halo):
    lane = iota((COND, LANES), 1)
    outer = (lane < REACH) | (lane >= LANES - REACH)
    return jnp.where(outer, halo[:COND], pltpu.roll(halo[COND:], LANES // 2, 1))


def unpack_halo(packed):
    return jnp.concatenate([packed, pltpu.roll(packed, LANES // 2, 1)], axis=0)


def join_halo(right, left):
    return jnp.where(iota((ROWS, LANES), 1) < LANES // 2, right, left)


def mirror_halo(first, last):
    lane = iota((COND, LANES), 1)
    back = LANES - 1 - lane

    def pick(tile, index):
        return jnp.take_along_axis(tile, index, axis=1)

    left_v = pick(first[:COND], back)
    left_i = jnp.where(lane == LANES - 1, 0.0, -pick(first[COND:], jnp.maximum(back - 1, 0)))
    right_v = jnp.where(lane == 0, 0.0, -pick(last[:COND], jnp.minimum(back + 1, LANES - 1)))
    right_i = pick(last[COND:], back)
    return jnp.concatenate([left_v, left_i], axis=0), jnp.concatenate([right_v, right_i], axis=0)


def make_halo(from_left, from_right, first, last):
    space = lax.axis_index("space")
    left, right = mirror_halo(first, last)
    halo = halo_of_edges(from_left, from_right)
    is_right = iota((ROWS, LANES), 1) < LANES // 2
    halo = jnp.where(is_right & (space == lax.axis_size("space") - 1), right, halo)
    return jnp.where(jnp.logical_not(is_right) & (space == 0), left, halo)


def split(state):
    high = state.astype(jnp.bfloat16)
    low = (state - high.astype(jnp.float32)).astype(jnp.bfloat16)
    return jnp.concatenate([high, high, low, high], axis=0)


def lower(added, current):
    return jnp.concatenate([added[:COND], added[COND:] + current], axis=0)


def multiply(weights, state):
    return jnp.dot(weights, split(state), preferred_element_type=jnp.float32)


def step(state, weights, width):
    return shift_once(multiply(weights, state), width)


def shift_once(product, width):
    outs = []
    for b in range(0, product.shape[1], width):
        e = b + width
        out = product[:ROWS, b:e] + pltpu.roll(product[ROWS : 2 * ROWS, b:e], 1, 1)
        outs.append(lower(out, pltpu.roll(product[2 * ROWS :, b:e], width - 1, 1)))
    return outs[0] if len(outs) == 1 else jnp.concatenate(outs, axis=1)


def shift_twice(product, width):
    outs = []
    for b in range(0, product.shape[1], width):
        e = b + width
        out = product[:ROWS, b:e]
        for m, shift in ((1, 1), (2, width - 1), (3, 2)):
            out = out + pltpu.roll(product[m * ROWS : (m + 1) * ROWS, b:e], shift, 1)
        outs.append(lower(out, pltpu.roll(product[4 * ROWS :, b:e], width - 2, 1)))
    return outs[0] if len(outs) == 1 else jnp.concatenate(outs, axis=1)


def tile_of(ref, k):
    return ref[:, k * LANES : (k + 1) * LANES]


def step_tiles(load, store, count, weights, ring, group):
    first = iota((ROWS, LANES), 1) == 0
    last = iota((COND, LANES), 1) == LANES - 1
    here, before, after = {}, {}, {}
    order = [count - 1, *range(count - 1)] if ring else list(range(count))
    for at in range(0, count, group):
        some = order[at : at + group]
        product = multiply(weights, jnp.concatenate([load(k) for k in some], axis=1))
        for j, k in enumerate(some):
            part = product[:, j * LANES : (j + 1) * LANES]
            here[k] = part[:ROWS]
            before[k] = pltpu.roll(part[ROWS : 2 * ROWS], 1, 1)
            after[k] = pltpu.roll(part[2 * ROWS :], LANES - 1, 1)
        for k in list(here):
            left, right = k - 1, k + 1
            if ring:
                left, right = left % count, right % count
            elif k == 0:
                left = k
            elif k == count - 1:
                right = k
            if left in before and right in after:
                tile = here.pop(k) + jnp.where(first, before[left], before[k])
                store(k, lower(tile, jnp.where(last, after[right], after[k])))


def prepare_kernel(fine_ref, coarse_ref, forcing_ref, out_ref, staged_ref, sem):
    copy = pltpu.make_async_copy(forcing_ref, staged_ref, sem)
    copy.start()

    def product(a, b):
        return jnp.dot(
            a, b, precision=lax.Precision.HIGHEST, preferred_element_type=jnp.float32
        )

    def put(at, whole):
        high = whole.astype(jnp.bfloat16)
        rest = whole - high.astype(jnp.float32)
        low = rest.astype(jnp.bfloat16)
        least = (rest - low.astype(jnp.float32)).astype(jnp.bfloat16)
        parts = jnp.concatenate([high, low, high, least], axis=1)
        out_ref[at : at + whole.shape[0], :] = parts

    for m, blocks_ref in enumerate((fine_ref, coarse_ref)):
        p_v, k_v, p_i, k_i = (blocks_ref[r] for r in range(4))
        k_pk = product(k_i, jnp.concatenate([p_v, k_v], axis=1))
        kp, kk = k_pk[:, :COND], k_pk[:, COND:]
        zero = jnp.zeros_like(kk)

        def block(a, b, c, d):
            top = jnp.concatenate([a, b], axis=1)
            return jnp.concatenate([top, jnp.concatenate([c, d], axis=1)], axis=0)

        own = block(p_v, -k_v, kp, p_i - 2.0 * kk)
        before = block(zero, k_v, zero, kk)
        after = block(zero, zero, -kp, kk)
        put(FINE if m == 0 else COARSE, jnp.concatenate([own, before, after[COND:]], axis=0))
        if m == 1:
            square = product(
                jnp.concatenate([own, before, after], axis=0),
                jnp.concatenate([own, before, after], axis=1),
            )

            def pair(a, b):
                return square[a * ROWS : (a + 1) * ROWS, b * ROWS : (b + 1) * ROWS]

            twice = [
                pair(0, 0) + pair(1, 2) + pair(2, 1),
                pair(0, 1) + pair(1, 0),
                pair(0, 2) + pair(2, 0),
                pair(1, 1),
                pair(2, 2)[COND:],
            ]
            put(COARSE_TWICE, jnp.concatenate(twice, axis=0))
    copy.wait()


def prepare(fine_blocks, coarse_blocks, forcing):
    vmem = pl.BlockSpec(memory_space=pltpu.VMEM)
    return pl.pallas_call(
        prepare_kernel,
        out_shape=(
            pltpu.VMEM((OPERATORS, 4 * ROWS), jnp.bfloat16),
            pltpu.VMEM(forcing.shape, jnp.float32),
        ),
        in_specs=[vmem, vmem, pl.BlockSpec(memory_space=pltpu.HBM)],
        out_specs=(vmem, vmem),
        scratch_shapes=[pltpu.SemaphoreType.DMA],
        compiler_params=pltpu.CompilerParams(vmem_limit_bytes=VMEM_LIMIT),
        name="prepare",
    )(fine_blocks, coarse_blocks, pltpu.with_memory_space_constraint(forcing, pltpu.HBM))


def edges_kernel(
    f_first, f_last, c_first, c_last, i_first, i_last, low_ref, high_ref, low_guess_ref, high_guess_ref
):
    count = f_first.shape[0]
    for n in range(count):
        low_ref[n] = pack_edge(f_first[n], 0)
        high_ref[n] = pack_edge(f_last[n], LANES - REACH)
    low_guess_ref[...] = pack_edge(c_first[0], 0)
    high_guess_ref[...] = pack_edge(c_last[0], LANES - REACH)
    low_ref[count] = low_guess_ref[...]
    high_ref[count] = high_guess_ref[...]
    low_ref[count + 1] = pack_edge(i_first[...], 0)
    high_ref[count + 1] = pack_edge(i_last[...], LANES - REACH)


def cut_edges(forcing, c_guess, initial):
    count, _, length = forcing.shape
    end = length // LANES - 1

    def both(shape, at):
        return [pl.BlockSpec(shape, lambda g, a=a: at(a)) for a in (0, end)]

    shape = jax.ShapeDtypeStruct((count + 2, 8, LANES), jnp.float32)
    whole = pl.BlockSpec(shape.shape, lambda g: (0, 0, 0))
    guess = jax.ShapeDtypeStruct((8, LANES), jnp.float32)
    whole_guess = pl.BlockSpec(guess.shape, lambda g: (0, 0))
    return pl.pallas_call(
        edges_kernel,
        grid=(1,),
        out_shape=(shape, shape, guess, guess),
        in_specs=both((count, ROWS, LANES), lambda a: (0, 0, a))
        + both((1, ROWS, LANES), lambda a: (0, 0, a))
        + both((ROWS, LANES), lambda a: (0, a)),
        out_specs=(whole, whole, whole_guess, whole_guess),
        name="edges",
    )(forcing, forcing, c_guess, c_guess, initial, initial)


def write_parts(out_ref, main, halo, at):
    groups = out_ref.shape[0]
    length = main.shape[1]
    part = length // groups
    tiles = part // LANES

    def tile(k):
        if k < 0 or k == length // LANES:
            return halo
        return main[:, k * LANES : (k + 1) * LANES]

    for j in range(groups):
        for i in range(tiles):
            out_ref[j, at + ROWS * i : at + ROWS * (i + 1), :] = tile(j * tiles + i)
        rim = join_halo(tile((j + 1) * tiles), tile(j * tiles - 1))
        out_ref[j, at + ROWS * tiles : at + ROWS * tiles + COND, :] = pack_halo(rim)


def source_halo_kernel(forcing_ref, left_ref, right_ref, halo_ref):
    count, _, length = forcing_ref.shape
    for n in range(count):
        halo_ref[n] = make_halo(
            left_ref[n], right_ref[n], forcing_ref[n, :, :LANES], forcing_ref[n, :, length - LANES :]
        )


def source_halos(forcing, left, right):
    vmem = pl.BlockSpec(memory_space=pltpu.VMEM)
    return pl.pallas_call(
        source_halo_kernel,
        out_shape=pltpu.VMEM((forcing.shape[0], ROWS, LANES), jnp.float32),
        in_specs=[vmem] * 3,
        out_specs=vmem,
        compiler_params=pltpu.CompilerParams(vmem_limit_bytes=VMEM_LIMIT),
        name="source_halos",
    )(forcing, left, right)


def start_chain(main_ref, begin_ref, initial_ref, sem):
    is_first = lax.axis_index("tm") == 0

    @pl.when(is_first)
    def _():
        pltpu.make_async_copy(initial_ref, main_ref, sem).start()

    @pl.when(jnp.logical_not(is_first))
    def _():
        pltpu.make_async_copy(begin_ref, main_ref, sem).start()

    return pltpu.make_async_copy(begin_ref, main_ref, sem)


def halo_of(main_ref, from_left, from_right):
    length = main_ref.shape[1]
    return make_halo(from_left, from_right, main_ref[:, :LANES], main_ref[:, length - LANES :])


def first_kernel(
    forcing_ref,
    source_halo_ref,
    begin_ref,
    initial_ref,
    guess_ref,
    left_ref,
    right_ref,
    begin_left_ref,
    begin_right_ref,
    weights_ref,
    out_ref,
    value_ref,
    own_ref,
    even_ref,
    odd_ref,
    sem,
):
    steps, _, length = forcing_ref.shape
    tiles = length // LANES
    guess_at, initial_at = left_ref.shape[0] - 2, left_ref.shape[0] - 1
    own = pltpu.make_async_copy(guess_ref.at[0], own_ref, sem)
    own.start()
    is_first = lax.axis_index("tm") == 0

    def begin(k):
        return jnp.where(is_first, tile_of(initial_ref, k), tile_of(begin_ref, k))

    begin_halo = make_halo(
        jnp.where(is_first, left_ref[initial_at], begin_left_ref[...]),
        jnp.where(is_first, right_ref[initial_at], begin_right_ref[...]),
        begin(0),
        begin(tiles - 1),
    )
    states = (even_ref, odd_ref)
    for n in range(steps):

        def load(k, n=n):
            if n > 0:
                return tile_of(states[n % 2], k)
            return begin(k - 1) if 0 < k <= tiles else begin_halo

        def store(k, tile, n=n):
            inside = 0 < k <= tiles
            tile = tile + (tile_of(forcing_ref.at[n], k - 1) if inside else source_halo_ref[n])
            if n == steps - 1 and inside:
                value_ref[:, (k - 1) * LANES : k * LANES] = tile
            else:
                states[(n + 1) % 2][:, k * LANES : (k + 1) * LANES] = tile

        step_tiles(load, store, tiles + 2, weights_ref[FINE:COARSE], False, 2)

    end = states[steps % 2]
    halo = join_halo(tile_of(end, tiles + 1), tile_of(end, 0))
    value_ref[:, length:] = halo
    own.wait()
    guess_halo = make_halo(
        left_ref[guess_at], right_ref[guess_at], tile_of(own_ref, 0), tile_of(own_ref, tiles - 1)
    )
    write_parts(out_ref, value_ref[:, :length] - own_ref[...], halo - guess_halo, 0)


def first_chain(
    forcing,
    source_halo,
    begin,
    initial,
    c_guess,
    left,
    right,
    begin_left,
    begin_right,
    weights,
    groups,
):
    steps, _, length = forcing.shape
    rows = length // groups // LANES * ROWS + COND
    anywhere = pl.BlockSpec(memory_space=pl.ANY)
    vmem = pl.BlockSpec(memory_space=pltpu.VMEM)
    return pl.pallas_call(
        first_kernel,
        out_shape=(
            pltpu.VMEM((groups, rows, LANES), jnp.float32),
            pltpu.VMEM((ROWS, length + LANES), jnp.float32),
        ),
        in_specs=[vmem, vmem, vmem, vmem, anywhere, vmem, vmem, vmem, vmem, vmem],
        out_specs=(vmem, vmem),
        scratch_shapes=[
            pltpu.VMEM((ROWS, length), jnp.float32),
            pltpu.VMEM((ROWS, length + 2 * LANES), jnp.float32),
            pltpu.VMEM((ROWS, length + 2 * LANES), jnp.float32),
            pltpu.SemaphoreType.DMA,
        ],
        compiler_params=pltpu.CompilerParams(vmem_limit_bytes=VMEM_LIMIT),
        cost_estimate=cost(steps, length, forcing.size),
        name="first_chain",
    )(
        forcing,
        source_halo,
        begin,
        initial,
        c_guess,
        left,
        right,
        begin_left,
        begin_right,
        weights,
    )


def cost(steps, columns, elements):
    return pl.CostEstimate(
        flops=steps * columns * 80 * 128 * 16, bytes_accessed=8 * elements, transcendentals=0
    )


def coarse_kernel(parts_ref, weights_ref, out_ref, even_ref, odd_ref):
    groups = parts_ref.shape[0]
    tiles = (parts_ref.shape[1] - COND) // ROWS
    width = (tiles + 1) * LANES

    states = (even_ref, odd_ref)
    for n in range(8):
        for t in range(groups - 1):

            def load(k, n=n, t=t):
                if n > 0:
                    return tile_of(states[n % 2], t * (tiles + 1) + k)
                if k < tiles:
                    return parts_ref[t, ROWS * k : ROWS * (k + 1), :]
                return unpack_halo(parts_ref[t, ROWS * tiles : ROWS * tiles + COND, :])

            def store(k, tile, n=n, t=t):
                at = t * width + k * LANES
                states[(n + 1) % 2][:, at : at + LANES] = tile

            step_tiles(load, store, tiles + 1, weights_ref[FINE:COARSE], True, tiles + 1)

    def put(t, ring):
        for i in range(tiles):
            out_ref[t, ROWS * i : ROWS * (i + 1), :] = ring[:, i * LANES : (i + 1) * LANES]

    resid = [even_ref[:, t * width : (t + 1) * width] for t in range(groups - 1)]
    second = range(1, groups - 2, 2)
    carried = step(
        jnp.concatenate([resid[t] for t in second], axis=1),
        weights_ref[COARSE:COARSE_TWICE],
        width,
    )
    out_ref[0] = jnp.zeros_like(out_ref[0])
    correction = resid[0]
    put(1, correction)
    for m, t in enumerate(second):
        both = multiply(weights_ref[COARSE:OPERATORS], correction)
        put(t + 1, shift_once(both[:ONCE], width) + resid[t])
        together = carried[:, m * width : (m + 1) * width] + resid[t + 1]
        correction = shift_twice(both[ONCE:], width) + together
        put(t + 2, correction)


def coarse_solve(parts, weights):
    groups, rows, _ = parts.shape
    tiles = (rows - COND) // ROWS
    return pl.pallas_call(
        coarse_kernel,
        out_shape=pltpu.VMEM((groups, ROWS * tiles, LANES), jnp.float32),
        scratch_shapes=[pltpu.VMEM((ROWS, (groups - 1) * (tiles + 1) * LANES), jnp.float32)] * 2,
        compiler_params=pltpu.CompilerParams(vmem_limit_bytes=VMEM_LIMIT),
        cost_estimate=cost(12, groups * tiles * LANES, parts.size),
        name="coarse_solve",
    )(parts, weights)


def second_kernel(
    forcing_ref,
    source_halo_ref,
    begin_ref,
    initial_ref,
    left_ref,
    right_ref,
    weights_ref,
    out_ref,
    states_ref,
    halo_ref,
    sems,
    out_sems,
):
    steps = out_sems.shape[0]
    length = forcing_ref.shape[2]
    initial_at = left_ref.shape[0] - 1
    halo = pltpu.make_async_copy(begin_ref.at[:, length:], halo_ref, sems.at[1])
    halo.start()
    begun = start_chain(states_ref.at[0], begin_ref.at[:, :length], initial_ref, sems.at[0])
    halo.wait()
    begun.wait()

    @pl.when(lax.axis_index("tm") == 0)
    def _():
        halo_ref[...] = halo_of(states_ref.at[0], left_ref[initial_at], right_ref[initial_at])

    def result(n):
        return pltpu.make_async_copy(states_ref.at[n + 1], out_ref.at[n], out_sems.at[n])

    def one(n, carry):
        state = jnp.concatenate([states_ref[n], halo_ref[...]], axis=1)
        state = step(state, weights_ref[FINE:COARSE], length + LANES)
        states_ref[n + 1] = state[:, :length] + forcing_ref[n]
        halo_ref[...] = state[:, length:] + source_halo_ref[n]
        result(n).start()
        return carry

    lax.fori_loop(0, steps, one, 0)
    for n in range(steps):
        result(n).wait()


def second_chain(forcing, source_halo, begin, initial, left, right, weights):
    count, _, length = forcing.shape
    hbm = pl.BlockSpec(memory_space=pltpu.HBM)
    anywhere = pl.BlockSpec(memory_space=pl.ANY)
    vmem = pl.BlockSpec(memory_space=pltpu.VMEM)
    return pl.pallas_call(
        second_kernel,
        out_shape=jax.ShapeDtypeStruct(forcing.shape, jnp.float32),
        in_specs=[vmem, vmem, anywhere, anywhere, vmem, vmem, vmem],
        out_specs=hbm,
        scratch_shapes=[
            pltpu.VMEM(forcing.shape, jnp.float32),
            pltpu.VMEM((ROWS, LANES), jnp.float32),
            pltpu.SemaphoreType.DMA((2,)),
            pltpu.SemaphoreType.DMA((count - 1,)),
        ],
        compiler_params=pltpu.CompilerParams(vmem_limit_bytes=VMEM_LIMIT),
        cost_estimate=cost(count, length, 2 * forcing.size),
        name="second_chain",
    )(forcing, source_halo, begin, initial, left, right, weights)


def correct_kernel(value_ref, parts_ref, states_ref, out_ref):
    del states_ref
    groups = parts_ref.shape[0]
    tiles = out_ref.shape[2] // groups // LANES
    for j in range(groups):
        for i in range(tiles):
            at = (j * tiles + i) * LANES
            out_ref[0, :, at : at + LANES] = (
                value_ref[:, at : at + LANES] + parts_ref[j, ROWS * i : ROWS * (i + 1), :]
            )


def correct_last(value, parts, states):
    count, _, length = states.shape
    return pl.pallas_call(
        correct_kernel,
        grid=(1,),
        out_shape=jax.ShapeDtypeStruct(states.shape, jnp.float32),
        in_specs=[
            pl.BlockSpec(value.shape, lambda g: (0, 0)),
            pl.BlockSpec(parts.shape, lambda g: (0, 0, 0)),
            pl.BlockSpec(memory_space=pl.ANY),
        ],
        out_specs=pl.BlockSpec((1, ROWS, length), lambda g: (count - 1, 0, 0)),
        input_output_aliases={2: 0},
        compiler_params=pltpu.CompilerParams(vmem_limit_bytes=VMEM_LIMIT),
        name="correct_last",
    )(value, parts, states)


def body(initial, c_guess, forcing, fine_blocks, coarse_blocks):
    groups = lax.axis_size("tm")
    spaces = lax.axis_size("space")
    up = [(i, (i + 1) % spaces) for i in range(spaces)]
    down = [(b, a) for a, b in up]
    to_next = [(i, (i + 1) % groups) for i in range(groups)]

    def to_next_and(pairs):
        return [(t * spaces + a, u * spaces + b) for t, u in to_next for a, b in pairs]

    begin = lax.ppermute(c_guess[0], "tm", to_next)
    low, high, low_guess, high_guess = cut_edges(forcing, c_guess, initial)
    right = lax.ppermute(low, "space", down)
    left = lax.ppermute(high, "space", up)
    begin_right = lax.ppermute(low_guess, ("tm", "space"), to_next_and(down))
    begin_left = lax.ppermute(high_guess, ("tm", "space"), to_next_and(up))
    weights, staged = prepare(fine_blocks, coarse_blocks, forcing)
    source_halo = source_halos(staged, left, right)
    parts, value = first_chain(
        staged,
        source_halo,
        begin,
        initial,
        c_guess,
        left,
        right,
        begin_left,
        begin_right,
        weights,
        groups,
    )
    parts = lax.all_to_all(parts, "tm", 0, 0, tiled=True)
    begin = lax.ppermute(value, "tm", to_next)
    parts = coarse_solve(parts, weights)
    parts = lax.all_to_all(parts, "tm", 0, 0, tiled=True)
    states = second_chain(staged, source_halo, begin, initial, left, right, weights)
    return correct_last(value, parts, states)


def solution(mesh):
    in_specs = (P(None, "space"), P("tm", None, "space"), P("tm", None, "space"), P(), P())
    out_specs = P("tm", None, "space")
    return jax.shard_map(body, mesh=mesh, in_specs=in_specs, out_specs=out_specs, check_vma=False)
```

```python
import jax
import jax.numpy as jnp
from jax import lax
from jax.experimental import pallas as pl
from jax.experimental.pallas import tpu as pltpu
from jax.sharding import PartitionSpec as P

LANES = 128
REACH = 32
RIM = 8
COND = 16
ROWS = 2 * COND
ONCE = 5 * COND
TWICE = 9 * COND
FINE, COARSE, COARSE_TWICE, OPERATORS = 0, ONCE, 2 * ONCE, 2 * ONCE + TWICE
AHEAD = 3
VMEM_LIMIT = 20 * 1024 * 1024


def iota(shape, axis):
    return lax.broadcasted_iota(jnp.int32, shape, axis)


def pack_edge(tile, base):
    lane = iota((8, LANES), 1)
    out = jnp.zeros((8, LANES), jnp.float32)
    for g in range(4):
        part = pltpu.roll(tile[8 * g : 8 * g + 8], (REACH * g - base) % LANES, 1)
        out = jnp.where(lane // REACH == g, part, out)
    return out


def unpack_edge(packed, base):
    return jnp.concatenate(
        [pltpu.roll(packed, (base - REACH * g) % LANES, 1) for g in range(4)], axis=0
    )


def halo_of_edges(from_left, from_right):
    lane = iota((ROWS, LANES), 1)
    right = jnp.where(lane < REACH, unpack_edge(from_right, 0), 0.0)
    return jnp.where(lane >= LANES - REACH, unpack_edge(from_left, LANES - REACH), right)


def join_halo(right, left):
    return jnp.where(iota((ROWS, LANES), 1) < LANES // 2, right, left)


def mirror_halo(first, last):
    lane = iota((COND, LANES), 1)
    back = LANES - 1 - lane

    def pick(tile, index):
        return jnp.take_along_axis(tile, index, axis=1)

    left_v = pick(first[:COND], back)
    left_i = jnp.where(lane == LANES - 1, 0.0, -pick(first[COND:], jnp.maximum(back - 1, 0)))
    right_v = jnp.where(lane == 0, 0.0, -pick(last[:COND], jnp.minimum(back + 1, LANES - 1)))
    right_i = pick(last[COND:], back)
    return jnp.concatenate([left_v, left_i], axis=0), jnp.concatenate([right_v, right_i], axis=0)


def make_halo(from_left, from_right, first, last):
    space = lax.axis_index("space")
    left, right = mirror_halo(first, last)
    halo = halo_of_edges(from_left, from_right)
    is_right = iota((ROWS, LANES), 1) < LANES // 2
    halo = jnp.where(is_right & (space == lax.axis_size("space") - 1), right, halo)
    return jnp.where(jnp.logical_not(is_right) & (space == 0), left, halo)


def split(state):
    high = state.astype(jnp.bfloat16)
    low = (state - high.astype(jnp.float32)).astype(jnp.bfloat16)
    return jnp.concatenate([high, high, low, high], axis=0)


def lower(added, current):
    return jnp.concatenate([added[:COND], added[COND:] + current], axis=0)


def multiply(weights, state):
    return jnp.dot(weights, split(state), preferred_element_type=jnp.float32)


def step(state, weights, width):
    return shift_once(multiply(weights, state), width)


def shift_once(product, width):
    outs = []
    for b in range(0, product.shape[1], width):
        e = b + width
        out = product[:ROWS, b:e] + pltpu.roll(product[ROWS : 2 * ROWS, b:e], 1, 1)
        outs.append(lower(out, pltpu.roll(product[2 * ROWS :, b:e], width - 1, 1)))
    return outs[0] if len(outs) == 1 else jnp.concatenate(outs, axis=1)


def shift_twice(product, width):
    outs = []
    for b in range(0, product.shape[1], width):
        e = b + width
        out = product[:ROWS, b:e]
        for m, shift in ((1, 1), (2, width - 1), (3, 2)):
            out = out + pltpu.roll(product[m * ROWS : (m + 1) * ROWS, b:e], shift, 1)
        outs.append(lower(out, pltpu.roll(product[4 * ROWS :, b:e], width - 2, 1)))
    return outs[0] if len(outs) == 1 else jnp.concatenate(outs, axis=1)


def tile_of(ref, k):
    return ref[:, k * LANES : (k + 1) * LANES]


def step_tiles(load, store, count, weights, ring, group):
    first = iota((ROWS, LANES), 1) == 0
    last = iota((COND, LANES), 1) == LANES - 1
    here, before, after = {}, {}, {}
    order = [count - 1, *range(count - 1)] if ring else list(range(count))
    for at in range(0, count, group):
        some = order[at : at + group]
        product = multiply(weights, jnp.concatenate([load(k) for k in some], axis=1))
        for j, k in enumerate(some):
            part = product[:, j * LANES : (j + 1) * LANES]
            here[k] = part[:ROWS]
            before[k] = pltpu.roll(part[ROWS : 2 * ROWS], 1, 1)
            after[k] = pltpu.roll(part[2 * ROWS :], LANES - 1, 1)
        for k in list(here):
            left, right = k - 1, k + 1
            if ring:
                left, right = left % count, right % count
            elif k == 0:
                left = k
            elif k == count - 1:
                right = k
            if left in before and right in after:
                tile = here.pop(k) + jnp.where(first, before[left], before[k])
                store(k, lower(tile, jnp.where(last, after[right], after[k])))


def prepare_kernel(fine_ref, coarse_ref, forcing_ref, out_ref, staged_ref, sem):
    copy = pltpu.make_async_copy(forcing_ref, staged_ref, sem)
    copy.start()

    def product(a, b):
        return jnp.dot(
            a, b, precision=lax.Precision.HIGHEST, preferred_element_type=jnp.float32
        )

    def put(at, whole):
        high = whole.astype(jnp.bfloat16)
        rest = whole - high.astype(jnp.float32)
        low = rest.astype(jnp.bfloat16)
        least = (rest - low.astype(jnp.float32)).astype(jnp.bfloat16)
        parts = jnp.concatenate([high, low, high, least], axis=1)
        out_ref[at : at + whole.shape[0], :] = parts

    for m, blocks_ref in enumerate((fine_ref, coarse_ref)):
        p_v, k_v, p_i, k_i = (blocks_ref[r] for r in range(4))
        k_pk = product(k_i, jnp.concatenate([p_v, k_v], axis=1))
        kp, kk = k_pk[:, :COND], k_pk[:, COND:]
        zero = jnp.zeros_like(kk)

        def block(a, b, c, d):
            top = jnp.concatenate([a, b], axis=1)
            return jnp.concatenate([top, jnp.concatenate([c, d], axis=1)], axis=0)

        own = block(p_v, -k_v, kp, p_i - 2.0 * kk)
        before = block(zero, k_v, zero, kk)
        after = block(zero, zero, -kp, kk)
        put(FINE if m == 0 else COARSE, jnp.concatenate([own, before, after[COND:]], axis=0))
        if m == 1:
            square = product(
                jnp.concatenate([own, before, after], axis=0),
                jnp.concatenate([own, before, after], axis=1),
            )

            def pair(a, b):
                return square[a * ROWS : (a + 1) * ROWS, b * ROWS : (b + 1) * ROWS]

            twice = [
                pair(0, 0) + pair(1, 2) + pair(2, 1),
                pair(0, 1) + pair(1, 0),
                pair(0, 2) + pair(2, 0),
                pair(1, 1),
                pair(2, 2)[COND:],
            ]
            put(COARSE_TWICE, jnp.concatenate(twice, axis=0))
    copy.wait()


def prepare(fine_blocks, coarse_blocks, forcing):
    vmem = pl.BlockSpec(memory_space=pltpu.VMEM)
    return pl.pallas_call(
        prepare_kernel,
        out_shape=(
            pltpu.VMEM((OPERATORS, 4 * ROWS), jnp.bfloat16),
            pltpu.VMEM(forcing.shape, jnp.float32),
        ),
        in_specs=[vmem, vmem, pl.BlockSpec(memory_space=pltpu.HBM)],
        out_specs=(vmem, vmem),
        scratch_shapes=[pltpu.SemaphoreType.DMA],
        compiler_params=pltpu.CompilerParams(vmem_limit_bytes=VMEM_LIMIT),
        name="prepare",
    )(fine_blocks, coarse_blocks, pltpu.with_memory_space_constraint(forcing, pltpu.HBM))


def edges_kernel(
    f_first, f_last, c_first, c_last, i_first, i_last, low_ref, high_ref, low_guess_ref, high_guess_ref
):
    count = f_first.shape[0]
    for n in range(count):
        low_ref[n] = pack_edge(f_first[n], 0)
        high_ref[n] = pack_edge(f_last[n], LANES - REACH)
    low_guess_ref[...] = pack_edge(c_first[0], 0)
    high_guess_ref[...] = pack_edge(c_last[0], LANES - REACH)
    low_ref[count] = low_guess_ref[...]
    high_ref[count] = high_guess_ref[...]
    low_ref[count + 1] = pack_edge(i_first[...], 0)
    high_ref[count + 1] = pack_edge(i_last[...], LANES - REACH)


def cut_edges(forcing, c_guess, initial):
    count, _, length = forcing.shape
    end = length // LANES - 1

    def both(shape, at):
        return [pl.BlockSpec(shape, lambda g, a=a: at(a)) for a in (0, end)]

    shape = jax.ShapeDtypeStruct((count + 2, 8, LANES), jnp.float32)
    whole = pl.BlockSpec(shape.shape, lambda g: (0, 0, 0))
    guess = jax.ShapeDtypeStruct((8, LANES), jnp.float32)
    whole_guess = pl.BlockSpec(guess.shape, lambda g: (0, 0))
    return pl.pallas_call(
        edges_kernel,
        grid=(1,),
        out_shape=(shape, shape, guess, guess),
        in_specs=both((count, ROWS, LANES), lambda a: (0, 0, a))
        + both((1, ROWS, LANES), lambda a: (0, 0, a))
        + both((ROWS, LANES), lambda a: (0, a)),
        out_specs=(whole, whole, whole_guess, whole_guess),
        name="edges",
    )(forcing, forcing, c_guess, c_guess, initial, initial)


def write_parts(out_ref, main, halo, at):
    groups = out_ref.shape[0]
    length = main.shape[1]
    part = length // groups
    tiles = part // LANES

    def tile(k):
        if k < 0 or k == length // LANES:
            return halo
        return main[:, k * LANES : (k + 1) * LANES]

    for j in range(groups):
        for i in range(tiles):
            out_ref[j, at + ROWS * i : at + ROWS * (i + 1), :] = tile(j * tiles + i)
        rim = join_halo(tile((j + 1) * tiles), tile(j * tiles - 1))
        out_ref[j, at + ROWS * tiles : at + ROWS * tiles + RIM, :] = pack_edge(rim, LANES - REACH // 2)


def source_halo_kernel(forcing_ref, left_ref, right_ref, halo_ref):
    count, _, length = forcing_ref.shape
    for n in range(count):
        halo_ref[n] = make_halo(
            left_ref[n], right_ref[n], forcing_ref[n, :, :LANES], forcing_ref[n, :, length - LANES :]
        )


def source_halos(forcing, left, right):
    vmem = pl.BlockSpec(memory_space=pltpu.VMEM)
    return pl.pallas_call(
        source_halo_kernel,
        out_shape=pltpu.VMEM((forcing.shape[0], ROWS, LANES), jnp.float32),
        in_specs=[vmem] * 3,
        out_specs=vmem,
        compiler_params=pltpu.CompilerParams(vmem_limit_bytes=VMEM_LIMIT),
        name="source_halos",
    )(forcing, left, right)


def first_kernel(
    forcing_ref,
    source_halo_ref,
    begin_ref,
    initial_ref,
    guess_ref,
    left_ref,
    right_ref,
    begin_left_ref,
    begin_right_ref,
    weights_ref,
    out_ref,
    value_ref,
    own_ref,
    even_ref,
    odd_ref,
    sem,
):
    steps, _, length = forcing_ref.shape
    tiles = length // LANES
    guess_at, initial_at = left_ref.shape[0] - 2, left_ref.shape[0] - 1
    own = pltpu.make_async_copy(guess_ref.at[0], own_ref, sem)
    own.start()
    is_first = lax.axis_index("tm") == 0

    def begin(k):
        return jnp.where(is_first, tile_of(initial_ref, k), tile_of(begin_ref, k))

    begin_halo = make_halo(
        jnp.where(is_first, left_ref[initial_at], begin_left_ref[...]),
        jnp.where(is_first, right_ref[initial_at], begin_right_ref[...]),
        begin(0),
        begin(tiles - 1),
    )
    states = (even_ref, odd_ref)
    for n in range(steps):

        def load(k, n=n):
            if n > 0:
                return tile_of(states[n % 2], k)
            return begin(k - 1) if 0 < k <= tiles else begin_halo

        def store(k, tile, n=n):
            inside = 0 < k <= tiles
            tile = tile + (tile_of(forcing_ref.at[n], k - 1) if inside else source_halo_ref[n])
            if n == steps - 1 and inside:
                value_ref[:, (k - 1) * LANES : k * LANES] = tile
            else:
                states[(n + 1) % 2][:, k * LANES : (k + 1) * LANES] = tile

        step_tiles(load, store, tiles + 2, weights_ref[FINE:COARSE], False, 2)

    end = states[steps % 2]
    halo = join_halo(tile_of(end, tiles + 1), tile_of(end, 0))
    value_ref[:, length:] = halo
    own.wait()
    guess_halo = make_halo(
        left_ref[guess_at], right_ref[guess_at], tile_of(own_ref, 0), tile_of(own_ref, tiles - 1)
    )
    write_parts(out_ref, value_ref[:, :length] - own_ref[...], halo - guess_halo, 0)


def first_chain(
    forcing,
    source_halo,
    begin,
    initial,
    c_guess,
    left,
    right,
    begin_left,
    begin_right,
    weights,
    groups,
):
    steps, _, length = forcing.shape
    rows = length // groups // LANES * ROWS + RIM
    anywhere = pl.BlockSpec(memory_space=pl.ANY)
    vmem = pl.BlockSpec(memory_space=pltpu.VMEM)
    return pl.pallas_call(
        first_kernel,
        out_shape=(
            pltpu.VMEM((groups, rows, LANES), jnp.float32),
            pltpu.VMEM((ROWS, length + LANES), jnp.float32),
        ),
        in_specs=[vmem, vmem, vmem, vmem, anywhere, vmem, vmem, vmem, vmem, vmem],
        out_specs=(vmem, vmem),
        scratch_shapes=[
            pltpu.VMEM((ROWS, length), jnp.float32),
            pltpu.VMEM((ROWS, length + 2 * LANES), jnp.float32),
            pltpu.VMEM((ROWS, length + 2 * LANES), jnp.float32),
            pltpu.SemaphoreType.DMA,
        ],
        compiler_params=pltpu.CompilerParams(vmem_limit_bytes=VMEM_LIMIT),
        cost_estimate=cost(steps, length, forcing.size),
        name="first_chain",
    )(
        forcing,
        source_halo,
        begin,
        initial,
        c_guess,
        left,
        right,
        begin_left,
        begin_right,
        weights,
    )


def cost(steps, columns, elements):
    return pl.CostEstimate(
        flops=steps * columns * 80 * 128 * 16, bytes_accessed=8 * elements, transcendentals=0
    )


def coarse_kernel(parts_ref, weights_ref, out_ref, even_ref, odd_ref):
    groups = parts_ref.shape[0]
    tiles = (parts_ref.shape[1] - RIM) // ROWS
    width = (tiles + 1) * LANES

    states = (even_ref, odd_ref)
    for n in range(8):
        for t in range(groups - 1):

            def load(k, n=n, t=t):
                if n > 0:
                    return tile_of(states[n % 2], t * (tiles + 1) + k)
                if k < tiles:
                    return parts_ref[t, ROWS * k : ROWS * (k + 1), :]
                return unpack_edge(parts_ref[t, ROWS * tiles : ROWS * tiles + RIM, :], LANES - REACH // 2)

            def store(k, tile, n=n, t=t):
                at = t * width + k * LANES
                states[(n + 1) % 2][:, at : at + LANES] = tile

            step_tiles(load, store, tiles + 1, weights_ref[FINE:COARSE], True, tiles + 1)

    def put(t, ring):
        for i in range(tiles):
            out_ref[t, ROWS * i : ROWS * (i + 1), :] = ring[:, i * LANES : (i + 1) * LANES]

    resid = [even_ref[:, t * width : (t + 1) * width] for t in range(groups - 1)]
    second = range(1, groups - 2, 2)
    carried = step(
        jnp.concatenate([resid[t] for t in second], axis=1),
        weights_ref[COARSE:COARSE_TWICE],
        width,
    )
    out_ref[0] = jnp.zeros_like(out_ref[0])
    correction = resid[0]
    put(1, correction)
    for m, t in enumerate(second):
        both = multiply(weights_ref[COARSE:OPERATORS], correction)
        put(t + 1, shift_once(both[:ONCE], width) + resid[t])
        together = carried[:, m * width : (m + 1) * width] + resid[t + 1]
        correction = shift_twice(both[ONCE:], width) + together
        put(t + 2, correction)


def coarse_solve(parts, weights):
    groups, rows, _ = parts.shape
    tiles = (rows - RIM) // ROWS
    return pl.pallas_call(
        coarse_kernel,
        out_shape=pltpu.VMEM((groups, ROWS * tiles, LANES), jnp.float32),
        scratch_shapes=[pltpu.VMEM((ROWS, (groups - 1) * (tiles + 1) * LANES), jnp.float32)] * 2,
        compiler_params=pltpu.CompilerParams(vmem_limit_bytes=VMEM_LIMIT),
        cost_estimate=cost(12, groups * tiles * LANES, parts.size),
        name="coarse_solve",
    )(parts, weights)


def second_kernel(
    forcing_ref,
    source_halo_ref,
    begin_ref,
    initial_ref,
    left_ref,
    right_ref,
    weights_ref,
    out_ref,
    states_ref,
    source_ref,
    low_ref,
    high_ref,
    source_sems,
    out_sems,
):
    steps = states_ref.shape[0]
    length = forcing_ref.shape[2]
    tiles = length // LANES
    initial_at = left_ref.shape[0] - 1
    is_first = lax.axis_index("tm") == 0

    def source(n):
        return pltpu.make_async_copy(forcing_ref.at[n], source_ref.at[n], source_sems.at[n])

    def result(n):
        return pltpu.make_async_copy(states_ref.at[n], out_ref.at[n], out_sems.at[n])

    for n in range(AHEAD):
        source(n).start()

    def begin(k):
        return jnp.where(is_first, tile_of(initial_ref, k), tile_of(begin_ref, k))

    begin_halo = jnp.where(
        is_first,
        make_halo(left_ref[initial_at], right_ref[initial_at], begin(0), begin(tiles - 1)),
        tile_of(begin_ref, tiles),
    )
    for n in range(steps):
        source(n).wait()
        if n + AHEAD < steps:
            source(n + AHEAD).start()

        def load(k, n=n):
            if 0 < k <= tiles:
                return tile_of(states_ref.at[n - 1], k - 1) if n > 0 else begin(k - 1)
            if n == 0:
                return begin_halo
            return low_ref[n - 1] if k == 0 else high_ref[n - 1]

        def store(k, tile, n=n):
            if 0 < k <= tiles:
                states_ref[n, :, (k - 1) * LANES : k * LANES] = tile + tile_of(source_ref.at[n], k - 1)
            elif k == 0:
                low_ref[n] = tile + source_halo_ref[n]
            else:
                high_ref[n] = tile + source_halo_ref[n]

        step_tiles(load, store, tiles + 2, weights_ref[FINE:COARSE], False, 2)
        result(n).start()
    for n in range(steps):
        result(n).wait()


def second_chain(forcing, source_halo, begin, initial, left, right, weights):
    count, _, length = forcing.shape
    steps = count - 1
    hbm = pl.BlockSpec(memory_space=pltpu.HBM)
    vmem = pl.BlockSpec(memory_space=pltpu.VMEM)
    return pl.pallas_call(
        second_kernel,
        out_shape=jax.ShapeDtypeStruct(forcing.shape, jnp.float32),
        in_specs=[hbm, vmem, vmem, vmem, vmem, vmem, vmem],
        out_specs=hbm,
        scratch_shapes=[
            pltpu.VMEM((steps, ROWS, length), jnp.float32),
            pltpu.VMEM((steps, ROWS, length), jnp.float32),
            pltpu.VMEM((steps, ROWS, LANES), jnp.float32),
            pltpu.VMEM((steps, ROWS, LANES), jnp.float32),
            pltpu.SemaphoreType.DMA((steps,)),
            pltpu.SemaphoreType.DMA((steps,)),
        ],
        compiler_params=pltpu.CompilerParams(vmem_limit_bytes=VMEM_LIMIT),
        cost_estimate=cost(count, length, 2 * forcing.size),
        name="second_chain",
    )(
        pltpu.with_memory_space_constraint(forcing, pltpu.HBM),
        source_halo,
        begin,
        initial,
        left,
        right,
        weights,
    )


def correct_kernel(value_ref, parts_ref, states_ref, out_ref):
    del states_ref
    groups = parts_ref.shape[0]
    tiles = out_ref.shape[2] // groups // LANES
    for j in range(groups):
        for i in range(tiles):
            at = (j * tiles + i) * LANES
            out_ref[0, :, at : at + LANES] = (
                value_ref[:, at : at + LANES] + parts_ref[j, ROWS * i : ROWS * (i + 1), :]
            )


def correct_last(value, parts, states):
    count, _, length = states.shape
    return pl.pallas_call(
        correct_kernel,
        grid=(1,),
        out_shape=jax.ShapeDtypeStruct(states.shape, jnp.float32),
        in_specs=[
            pl.BlockSpec(value.shape, lambda g: (0, 0)),
            pl.BlockSpec(parts.shape, lambda g: (0, 0, 0)),
            pl.BlockSpec(memory_space=pl.ANY),
        ],
        out_specs=pl.BlockSpec((1, ROWS, length), lambda g: (count - 1, 0, 0)),
        input_output_aliases={2: 0},
        compiler_params=pltpu.CompilerParams(vmem_limit_bytes=VMEM_LIMIT),
        name="correct_last",
    )(value, parts, states)


def body(initial, c_guess, forcing, fine_blocks, coarse_blocks):
    groups = lax.axis_size("tm")
    spaces = lax.axis_size("space")
    up = [(i, (i + 1) % spaces) for i in range(spaces)]
    down = [(b, a) for a, b in up]
    to_next = [(i, (i + 1) % groups) for i in range(groups)]

    def to_next_and(pairs):
        return [(t * spaces + a, u * spaces + b) for t, u in to_next for a, b in pairs]

    begin = lax.ppermute(c_guess[0], "tm", to_next)
    low, high, low_guess, high_guess = cut_edges(forcing, c_guess, initial)
    right = lax.ppermute(low, "space", down)
    left = lax.ppermute(high, "space", up)
    begin_right = lax.ppermute(low_guess, ("tm", "space"), to_next_and(down))
    begin_left = lax.ppermute(high_guess, ("tm", "space"), to_next_and(up))
    weights, staged = prepare(fine_blocks, coarse_blocks, forcing)
    source_halo = source_halos(staged, left, right)
    parts, value = first_chain(
        staged,
        source_halo,
        begin,
        initial,
        c_guess,
        left,
        right,
        begin_left,
        begin_right,
        weights,
        groups,
    )
    parts = lax.all_to_all(parts, "tm", 0, 0, tiled=True)
    begin = lax.ppermute(value, "tm", to_next)
    parts = coarse_solve(parts, weights)
    parts = lax.all_to_all(parts, "tm", 0, 0, tiled=True)
    states = second_chain(forcing, source_halo, begin, initial, left, right, weights)
    return correct_last(value, parts, states)


def solution(mesh):
    in_specs = (P(None, "space"), P("tm", None, "space"), P("tm", None, "space"), P(), P())
    out_specs = P("tm", None, "space")
    return jax.shard_map(body, mesh=mesh, in_specs=in_specs, out_specs=out_specs, check_vma=False)
```

```python
import jax
import jax.numpy as jnp
from jax import lax
from jax.experimental import pallas as pl
from jax.experimental.pallas import tpu as pltpu
from jax.sharding import PartitionSpec as P

LANES = 128
REACH = 32
RIM = 8
COND = 16
ROWS = 2 * COND
ONCE = 5 * COND
TWICE = 9 * COND
FINE, COARSE, COARSE_TWICE, OPERATORS = 0, ONCE, 2 * ONCE, 2 * ONCE + TWICE
AHEAD = 3
VMEM_LIMIT = 20 * 1024 * 1024


def iota(shape, axis):
    return lax.broadcasted_iota(jnp.int32, shape, axis)


def pack_edge(tile, base):
    lane = iota((8, LANES), 1)
    out = jnp.zeros((8, LANES), jnp.float32)
    for g in range(4):
        part = pltpu.roll(tile[8 * g : 8 * g + 8], (REACH * g - base) % LANES, 1)
        out = jnp.where(lane // REACH == g, part, out)
    return out


def unpack_edge(packed, base):
    return jnp.concatenate(
        [pltpu.roll(packed, (base - REACH * g) % LANES, 1) for g in range(4)], axis=0
    )


def halo_of_edges(from_left, from_right):
    lane = iota((ROWS, LANES), 1)
    right = jnp.where(lane < REACH, unpack_edge(from_right, 0), 0.0)
    return jnp.where(lane >= LANES - REACH, unpack_edge(from_left, LANES - REACH), right)


def join_halo(right, left):
    return jnp.where(iota((ROWS, LANES), 1) < LANES // 2, right, left)


def mirror_halo(first, last):
    lane = iota((COND, LANES), 1)
    back = LANES - 1 - lane

    def pick(tile, index):
        return jnp.take_along_axis(tile, index, axis=1)

    left_v = pick(first[:COND], back)
    left_i = jnp.where(lane == LANES - 1, 0.0, -pick(first[COND:], jnp.maximum(back - 1, 0)))
    right_v = jnp.where(lane == 0, 0.0, -pick(last[:COND], jnp.minimum(back + 1, LANES - 1)))
    right_i = pick(last[COND:], back)
    return jnp.concatenate([left_v, left_i], axis=0), jnp.concatenate([right_v, right_i], axis=0)


def make_halo(from_left, from_right, first, last):
    space = lax.axis_index("space")
    left, right = mirror_halo(first, last)
    halo = halo_of_edges(from_left, from_right)
    is_right = iota((ROWS, LANES), 1) < LANES // 2
    halo = jnp.where(is_right & (space == lax.axis_size("space") - 1), right, halo)
    return jnp.where(jnp.logical_not(is_right) & (space == 0), left, halo)


def split(state):
    high = state.astype(jnp.bfloat16)
    low = (state - high.astype(jnp.float32)).astype(jnp.bfloat16)
    return jnp.concatenate([high, high, low, high], axis=0)


def lower(added, current):
    return jnp.concatenate([added[:COND], added[COND:] + current], axis=0)


def multiply(weights, state):
    return jnp.dot(weights, split(state), preferred_element_type=jnp.float32)


def step(state, weights, width):
    return shift_once(multiply(weights, state), width)


def shift_once(product, width):
    outs = []
    for b in range(0, product.shape[1], width):
        e = b + width
        out = product[:ROWS, b:e] + pltpu.roll(product[ROWS : 2 * ROWS, b:e], 1, 1)
        outs.append(lower(out, pltpu.roll(product[2 * ROWS :, b:e], width - 1, 1)))
    return outs[0] if len(outs) == 1 else jnp.concatenate(outs, axis=1)


def shift_twice(product, width):
    outs = []
    for b in range(0, product.shape[1], width):
        e = b + width
        out = product[:ROWS, b:e]
        for m, shift in ((1, 1), (2, width - 1), (3, 2)):
            out = out + pltpu.roll(product[m * ROWS : (m + 1) * ROWS, b:e], shift, 1)
        outs.append(lower(out, pltpu.roll(product[4 * ROWS :, b:e], width - 2, 1)))
    return outs[0] if len(outs) == 1 else jnp.concatenate(outs, axis=1)


def tile_of(ref, k):
    return ref[:, k * LANES : (k + 1) * LANES]


def step_tiles(load, store, count, weights, ring, group):
    first = iota((ROWS, LANES), 1) == 0
    last = iota((COND, LANES), 1) == LANES - 1
    here, before, after = {}, {}, {}
    order = [count - 1, *range(count - 1)] if ring else list(range(count))
    for at in range(0, count, group):
        some = order[at : at + group]
        product = multiply(weights, jnp.concatenate([load(k) for k in some], axis=1))
        for j, k in enumerate(some):
            part = product[:, j * LANES : (j + 1) * LANES]
            here[k] = part[:ROWS]
            before[k] = pltpu.roll(part[ROWS : 2 * ROWS], 1, 1)
            after[k] = pltpu.roll(part[2 * ROWS :], LANES - 1, 1)
        for k in list(here):
            left, right = k - 1, k + 1
            if ring:
                left, right = left % count, right % count
            elif k == 0:
                left = k
            elif k == count - 1:
                right = k
            if left in before and right in after:
                tile = here.pop(k) + jnp.where(first, before[left], before[k])
                store(k, lower(tile, jnp.where(last, after[right], after[k])))


def prepare_kernel(fine_ref, coarse_ref, forcing_ref, out_ref, staged_ref, sem):
    copy = pltpu.make_async_copy(forcing_ref, staged_ref, sem)
    copy.start()

    def product(a, b):
        return jnp.dot(
            a, b, precision=lax.Precision.HIGHEST, preferred_element_type=jnp.float32
        )

    def put(at, whole):
        high = whole.astype(jnp.bfloat16)
        rest = whole - high.astype(jnp.float32)
        low = rest.astype(jnp.bfloat16)
        least = (rest - low.astype(jnp.float32)).astype(jnp.bfloat16)
        parts = jnp.concatenate([high, low, high, least], axis=1)
        out_ref[at : at + whole.shape[0], :] = parts

    for m, blocks_ref in enumerate((fine_ref, coarse_ref)):
        p_v, k_v, p_i, k_i = (blocks_ref[r] for r in range(4))
        k_pk = product(k_i, jnp.concatenate([p_v, k_v], axis=1))
        kp, kk = k_pk[:, :COND], k_pk[:, COND:]
        zero = jnp.zeros_like(kk)

        def block(a, b, c, d):
            top = jnp.concatenate([a, b], axis=1)
            return jnp.concatenate([top, jnp.concatenate([c, d], axis=1)], axis=0)

        own = block(p_v, -k_v, kp, p_i - 2.0 * kk)
        before = block(zero, k_v, zero, kk)
        after = block(zero, zero, -kp, kk)
        put(FINE if m == 0 else COARSE, jnp.concatenate([own, before, after[COND:]], axis=0))
        if m == 1:
            square = product(
                jnp.concatenate([own, before, after], axis=0),
                jnp.concatenate([own, before, after], axis=1),
            )

            def pair(a, b):
                return square[a * ROWS : (a + 1) * ROWS, b * ROWS : (b + 1) * ROWS]

            twice = [
                pair(0, 0) + pair(1, 2) + pair(2, 1),
                pair(0, 1) + pair(1, 0),
                pair(0, 2) + pair(2, 0),
                pair(1, 1),
                pair(2, 2)[COND:],
            ]
            put(COARSE_TWICE, jnp.concatenate(twice, axis=0))
    copy.wait()


def prepare(fine_blocks, coarse_blocks, forcing):
    vmem = pl.BlockSpec(memory_space=pltpu.VMEM)
    return pl.pallas_call(
        prepare_kernel,
        out_shape=(
            pltpu.VMEM((OPERATORS, 4 * ROWS), jnp.bfloat16),
            pltpu.VMEM(forcing.shape, jnp.float32),
        ),
        in_specs=[vmem, vmem, pl.BlockSpec(memory_space=pltpu.HBM)],
        out_specs=(vmem, vmem),
        scratch_shapes=[pltpu.SemaphoreType.DMA],
        compiler_params=pltpu.CompilerParams(vmem_limit_bytes=VMEM_LIMIT),
        name="prepare",
    )(fine_blocks, coarse_blocks, pltpu.with_memory_space_constraint(forcing, pltpu.HBM))


def edges_kernel(
    f_first, f_last, c_first, c_last, i_first, i_last, low_ref, high_ref, low_guess_ref, high_guess_ref
):
    count = f_first.shape[0]
    for n in range(count):
        low_ref[n] = pack_edge(f_first[n], 0)
        high_ref[n] = pack_edge(f_last[n], LANES - REACH)
    low_guess_ref[...] = pack_edge(c_first[0], 0)
    high_guess_ref[...] = pack_edge(c_last[0], LANES - REACH)
    low_ref[count] = low_guess_ref[...]
    high_ref[count] = high_guess_ref[...]
    low_ref[count + 1] = pack_edge(i_first[...], 0)
    high_ref[count + 1] = pack_edge(i_last[...], LANES - REACH)


def cut_edges(forcing, c_guess, initial):
    count, _, length = forcing.shape
    end = length // LANES - 1

    def both(shape, at):
        return [pl.BlockSpec(shape, lambda g, a=a: at(a)) for a in (0, end)]

    shape = jax.ShapeDtypeStruct((count + 2, 8, LANES), jnp.float32)
    whole = pl.BlockSpec(shape.shape, lambda g: (0, 0, 0))
    guess = jax.ShapeDtypeStruct((8, LANES), jnp.float32)
    whole_guess = pl.BlockSpec(guess.shape, lambda g: (0, 0))
    return pl.pallas_call(
        edges_kernel,
        grid=(1,),
        out_shape=(shape, shape, guess, guess),
        in_specs=both((count, ROWS, LANES), lambda a: (0, 0, a))
        + both((1, ROWS, LANES), lambda a: (0, 0, a))
        + both((ROWS, LANES), lambda a: (0, a)),
        out_specs=(whole, whole, whole_guess, whole_guess),
        name="edges",
    )(forcing, forcing, c_guess, c_guess, initial, initial)


def write_parts(out_ref, main, halo, at):
    groups = out_ref.shape[0]
    length = main.shape[1]
    part = length // groups
    tiles = part // LANES

    def tile(k):
        if k < 0 or k == length // LANES:
            return halo
        return main[:, k * LANES : (k + 1) * LANES]

    for j in range(groups):
        for i in range(tiles):
            out_ref[j, at + ROWS * i : at + ROWS * (i + 1), :] = tile(j * tiles + i)
        rim = join_halo(tile((j + 1) * tiles), tile(j * tiles - 1))
        out_ref[j, at + ROWS * tiles : at + ROWS * tiles + RIM, :] = pack_edge(rim, LANES - REACH // 2)


def source_halo_kernel(forcing_ref, left_ref, right_ref, halo_ref):
    count, _, length = forcing_ref.shape
    for n in range(count):
        halo_ref[n] = make_halo(
            left_ref[n], right_ref[n], forcing_ref[n, :, :LANES], forcing_ref[n, :, length - LANES :]
        )


def source_halos(forcing, left, right):
    vmem = pl.BlockSpec(memory_space=pltpu.VMEM)
    return pl.pallas_call(
        source_halo_kernel,
        out_shape=pltpu.VMEM((forcing.shape[0], ROWS, LANES), jnp.float32),
        in_specs=[vmem] * 3,
        out_specs=vmem,
        compiler_params=pltpu.CompilerParams(vmem_limit_bytes=VMEM_LIMIT),
        name="source_halos",
    )(forcing, left, right)


def first_kernel(
    forcing_ref,
    source_halo_ref,
    begin_ref,
    initial_ref,
    guess_ref,
    left_ref,
    right_ref,
    begin_left_ref,
    begin_right_ref,
    weights_ref,
    out_ref,
    value_ref,
    own_ref,
    even_ref,
    odd_ref,
    sem,
):
    steps, _, length = forcing_ref.shape
    tiles = length // LANES
    guess_at, initial_at = left_ref.shape[0] - 2, left_ref.shape[0] - 1
    own = pltpu.make_async_copy(guess_ref.at[0], own_ref, sem)
    own.start()
    is_first = lax.axis_index("tm") == 0

    def begin(k):
        return jnp.where(is_first, tile_of(initial_ref, k), tile_of(begin_ref, k))

    begin_halo = make_halo(
        jnp.where(is_first, left_ref[initial_at], begin_left_ref[...]),
        jnp.where(is_first, right_ref[initial_at], begin_right_ref[...]),
        begin(0),
        begin(tiles - 1),
    )
    states = (even_ref, odd_ref)
    for n in range(steps):

        def load(k, n=n):
            if n > 0:
                return tile_of(states[n % 2], k)
            return begin(k - 1) if 0 < k <= tiles else begin_halo

        def store(k, tile, n=n):
            inside = 0 < k <= tiles
            tile = tile + (tile_of(forcing_ref.at[n], k - 1) if inside else source_halo_ref[n])
            if n == steps - 1 and inside:
                value_ref[:, (k - 1) * LANES : k * LANES] = tile
            else:
                states[(n + 1) % 2][:, k * LANES : (k + 1) * LANES] = tile

        step_tiles(load, store, tiles + 2, weights_ref[FINE:COARSE], False, 3)

    end = states[steps % 2]
    halo = join_halo(tile_of(end, tiles + 1), tile_of(end, 0))
    value_ref[:, length:] = halo
    own.wait()
    guess_halo = make_halo(
        left_ref[guess_at], right_ref[guess_at], tile_of(own_ref, 0), tile_of(own_ref, tiles - 1)
    )
    write_parts(out_ref, value_ref[:, :length] - own_ref[...], halo - guess_halo, 0)


def first_chain(
    forcing,
    source_halo,
    begin,
    initial,
    c_guess,
    left,
    right,
    begin_left,
    begin_right,
    weights,
    groups,
):
    steps, _, length = forcing.shape
    rows = length // groups // LANES * ROWS + RIM
    anywhere = pl.BlockSpec(memory_space=pl.ANY)
    vmem = pl.BlockSpec(memory_space=pltpu.VMEM)
    return pl.pallas_call(
        first_kernel,
        out_shape=(
            pltpu.VMEM((groups, rows, LANES), jnp.float32),
            pltpu.VMEM((ROWS, length + LANES), jnp.float32),
        ),
        in_specs=[vmem, vmem, vmem, vmem, anywhere, vmem, vmem, vmem, vmem, vmem],
        out_specs=(vmem, vmem),
        scratch_shapes=[
            pltpu.VMEM((ROWS, length), jnp.float32),
            pltpu.VMEM((ROWS, length + 2 * LANES), jnp.float32),
            pltpu.VMEM((ROWS, length + 2 * LANES), jnp.float32),
            pltpu.SemaphoreType.DMA,
        ],
        compiler_params=pltpu.CompilerParams(vmem_limit_bytes=VMEM_LIMIT),
        cost_estimate=cost(steps, length, forcing.size),
        name="first_chain",
    )(
        forcing,
        source_halo,
        begin,
        initial,
        c_guess,
        left,
        right,
        begin_left,
        begin_right,
        weights,
    )


def cost(steps, columns, elements):
    return pl.CostEstimate(
        flops=steps * columns * 80 * 128 * 16, bytes_accessed=8 * elements, transcendentals=0
    )


def coarse_kernel(parts_ref, weights_ref, out_ref, even_ref, odd_ref):
    groups = parts_ref.shape[0]
    tiles = (parts_ref.shape[1] - RIM) // ROWS
    width = (tiles + 1) * LANES

    states = (even_ref, odd_ref)
    for n in range(8):
        for t in range(groups - 1):

            def load(k, n=n, t=t):
                if n > 0:
                    return tile_of(states[n % 2], t * (tiles + 1) + k)
                if k < tiles:
                    return parts_ref[t, ROWS * k : ROWS * (k + 1), :]
                return unpack_edge(parts_ref[t, ROWS * tiles : ROWS * tiles + RIM, :], LANES - REACH // 2)

            def store(k, tile, n=n, t=t):
                at = t * width + k * LANES
                states[(n + 1) % 2][:, at : at + LANES] = tile

            step_tiles(load, store, tiles + 1, weights_ref[FINE:COARSE], True, tiles + 1)

    def put(t, ring):
        for i in range(tiles):
            out_ref[t, ROWS * i : ROWS * (i + 1), :] = ring[:, i * LANES : (i + 1) * LANES]

    resid = [even_ref[:, t * width : (t + 1) * width] for t in range(groups - 1)]
    second = range(1, groups - 2, 2)
    carried = step(
        jnp.concatenate([resid[t] for t in second], axis=1),
        weights_ref[COARSE:COARSE_TWICE],
        width,
    )
    out_ref[0] = jnp.zeros_like(out_ref[0])
    correction = resid[0]
    put(1, correction)
    for m, t in enumerate(second):
        both = multiply(weights_ref[COARSE:OPERATORS], correction)
        put(t + 1, shift_once(both[:ONCE], width) + resid[t])
        together = carried[:, m * width : (m + 1) * width] + resid[t + 1]
        correction = shift_twice(both[ONCE:], width) + together
        put(t + 2, correction)


def coarse_solve(parts, weights):
    groups, rows, _ = parts.shape
    tiles = (rows - RIM) // ROWS
    return pl.pallas_call(
        coarse_kernel,
        out_shape=pltpu.VMEM((groups, ROWS * tiles, LANES), jnp.float32),
        scratch_shapes=[pltpu.VMEM((ROWS, (groups - 1) * (tiles + 1) * LANES), jnp.float32)] * 2,
        compiler_params=pltpu.CompilerParams(vmem_limit_bytes=VMEM_LIMIT),
        cost_estimate=cost(12, groups * tiles * LANES, parts.size),
        name="coarse_solve",
    )(parts, weights)


def second_kernel(
    forcing_ref,
    source_halo_ref,
    begin_ref,
    initial_ref,
    left_ref,
    right_ref,
    weights_ref,
    out_ref,
    states_ref,
    source_ref,
    low_ref,
    high_ref,
    source_sems,
    out_sems,
):
    steps = states_ref.shape[0]
    length = forcing_ref.shape[2]
    tiles = length // LANES
    initial_at = left_ref.shape[0] - 1
    is_first = lax.axis_index("tm") == 0

    def source(n):
        return pltpu.make_async_copy(forcing_ref.at[n], source_ref.at[n], source_sems.at[n])

    def result(n):
        return pltpu.make_async_copy(states_ref.at[n], out_ref.at[n], out_sems.at[n])

    for n in range(AHEAD):
        source(n).start()

    def begin(k):
        return jnp.where(is_first, tile_of(initial_ref, k), tile_of(begin_ref, k))

    begin_halo = jnp.where(
        is_first,
        make_halo(left_ref[initial_at], right_ref[initial_at], begin(0), begin(tiles - 1)),
        tile_of(begin_ref, tiles),
    )
    for n in range(steps):
        source(n).wait()
        if n + AHEAD < steps:
            source(n + AHEAD).start()

        def load(k, n=n):
            if 0 < k <= tiles:
                return tile_of(states_ref.at[n - 1], k - 1) if n > 0 else begin(k - 1)
            if n == 0:
                return begin_halo
            return low_ref[n - 1] if k == 0 else high_ref[n - 1]

        def store(k, tile, n=n):
            if 0 < k <= tiles:
                states_ref[n, :, (k - 1) * LANES : k * LANES] = tile + tile_of(source_ref.at[n], k - 1)
            elif k == 0:
                low_ref[n] = tile + source_halo_ref[n]
            else:
                high_ref[n] = tile + source_halo_ref[n]

        step_tiles(load, store, tiles + 2, weights_ref[FINE:COARSE], False, 3)
        result(n).start()
    for n in range(steps):
        result(n).wait()


def second_chain(forcing, source_halo, begin, initial, left, right, weights):
    count, _, length = forcing.shape
    steps = count - 1
    hbm = pl.BlockSpec(memory_space=pltpu.HBM)
    vmem = pl.BlockSpec(memory_space=pltpu.VMEM)
    return pl.pallas_call(
        second_kernel,
        out_shape=jax.ShapeDtypeStruct(forcing.shape, jnp.float32),
        in_specs=[hbm, vmem, vmem, vmem, vmem, vmem, vmem],
        out_specs=hbm,
        scratch_shapes=[
            pltpu.VMEM((steps, ROWS, length), jnp.float32),
            pltpu.VMEM((steps, ROWS, length), jnp.float32),
            pltpu.VMEM((steps, ROWS, LANES), jnp.float32),
            pltpu.VMEM((steps, ROWS, LANES), jnp.float32),
            pltpu.SemaphoreType.DMA((steps,)),
            pltpu.SemaphoreType.DMA((steps,)),
        ],
        compiler_params=pltpu.CompilerParams(vmem_limit_bytes=VMEM_LIMIT),
        cost_estimate=cost(count, length, 2 * forcing.size),
        name="second_chain",
    )(
        pltpu.with_memory_space_constraint(forcing, pltpu.HBM),
        source_halo,
        begin,
        initial,
        left,
        right,
        weights,
    )


def correct_kernel(value_ref, parts_ref, states_ref, out_ref):
    del states_ref
    groups = parts_ref.shape[0]
    tiles = out_ref.shape[2] // groups // LANES
    for j in range(groups):
        for i in range(tiles):
            at = (j * tiles + i) * LANES
            out_ref[0, :, at : at + LANES] = (
                value_ref[:, at : at + LANES] + parts_ref[j, ROWS * i : ROWS * (i + 1), :]
            )


def correct_last(value, parts, states):
    count, _, length = states.shape
    return pl.pallas_call(
        correct_kernel,
        grid=(1,),
        out_shape=jax.ShapeDtypeStruct(states.shape, jnp.float32),
        in_specs=[
            pl.BlockSpec(value.shape, lambda g: (0, 0)),
            pl.BlockSpec(parts.shape, lambda g: (0, 0, 0)),
            pl.BlockSpec(memory_space=pl.ANY),
        ],
        out_specs=pl.BlockSpec((1, ROWS, length), lambda g: (count - 1, 0, 0)),
        input_output_aliases={2: 0},
        compiler_params=pltpu.CompilerParams(vmem_limit_bytes=VMEM_LIMIT),
        name="correct_last",
    )(value, parts, states)


def body(initial, c_guess, forcing, fine_blocks, coarse_blocks):
    groups = lax.axis_size("tm")
    spaces = lax.axis_size("space")
    up = [(i, (i + 1) % spaces) for i in range(spaces)]
    down = [(b, a) for a, b in up]
    to_next = [(i, (i + 1) % groups) for i in range(groups)]

    def to_next_and(pairs):
        return [(t * spaces + a, u * spaces + b) for t, u in to_next for a, b in pairs]

    begin = lax.ppermute(c_guess[0], "tm", to_next)
    low, high, low_guess, high_guess = cut_edges(forcing, c_guess, initial)
    right = lax.ppermute(low, "space", down)
    left = lax.ppermute(high, "space", up)
    begin_right = lax.ppermute(low_guess, ("tm", "space"), to_next_and(down))
    begin_left = lax.ppermute(high_guess, ("tm", "space"), to_next_and(up))
    weights, staged = prepare(fine_blocks, coarse_blocks, forcing)
    source_halo = source_halos(staged, left, right)
    parts, value = first_chain(
        staged,
        source_halo,
        begin,
        initial,
        c_guess,
        left,
        right,
        begin_left,
        begin_right,
        weights,
        groups,
    )
    parts = lax.all_to_all(parts, "tm", 0, 0, tiled=True)
    begin = lax.ppermute(value, "tm", to_next[:-1])
    parts = coarse_solve(parts, weights)
    parts = lax.all_to_all(parts, "tm", 0, 0, tiled=True)
    states = second_chain(forcing, source_halo, begin, initial, left, right, weights)
    return correct_last(value, parts, states)


def solution(mesh):
    in_specs = (P(None, "space"), P("tm", None, "space"), P("tm", None, "space"), P(), P())
    out_specs = P("tm", None, "space")
    return jax.shard_map(body, mesh=mesh, in_specs=in_specs, out_specs=out_specs, check_vma=False)
```

```python
import jax
import jax.numpy as jnp
from jax import lax
from jax.experimental import pallas as pl
from jax.experimental.pallas import tpu as pltpu
from jax.sharding import PartitionSpec as P

LANES = 128
REACH = 32
RIM = 8
COND = 16
ROWS = 2 * COND
ONCE = 5 * COND
TWICE = 9 * COND
FINE, COARSE, COARSE_TWICE, OPERATORS = 0, ONCE, 2 * ONCE, 2 * ONCE + TWICE
AHEAD = 3
VMEM_LIMIT = 20 * 1024 * 1024


def iota(shape, axis):
    return lax.broadcasted_iota(jnp.int32, shape, axis)


def pack_edge(tile, base):
    lane = iota((8, LANES), 1)
    out = jnp.zeros((8, LANES), jnp.float32)
    for g in range(4):
        part = pltpu.roll(tile[8 * g : 8 * g + 8], (REACH * g - base) % LANES, 1)
        out = jnp.where(lane // REACH == g, part, out)
    return out


def unpack_edge(packed, base):
    return jnp.concatenate(
        [pltpu.roll(packed, (base - REACH * g) % LANES, 1) for g in range(4)], axis=0
    )


def halo_of_edges(from_left, from_right):
    lane = iota((ROWS, LANES), 1)
    right = jnp.where(lane < REACH, unpack_edge(from_right, 0), 0.0)
    return jnp.where(lane >= LANES - REACH, unpack_edge(from_left, LANES - REACH), right)


def join_halo(right, left):
    return jnp.where(iota((ROWS, LANES), 1) < LANES // 2, right, left)


def mirror_halo(first, last):
    lane = iota((COND, LANES), 1)
    back = LANES - 1 - lane

    def pick(tile, index):
        return jnp.take_along_axis(tile, index, axis=1)

    left_v = pick(first[:COND], back)
    left_i = jnp.where(lane == LANES - 1, 0.0, -pick(first[COND:], jnp.maximum(back - 1, 0)))
    right_v = jnp.where(lane == 0, 0.0, -pick(last[:COND], jnp.minimum(back + 1, LANES - 1)))
    right_i = pick(last[COND:], back)
    return jnp.concatenate([left_v, left_i], axis=0), jnp.concatenate([right_v, right_i], axis=0)


def make_halo(from_left, from_right, first, last):
    space = lax.axis_index("space")
    left, right = mirror_halo(first, last)
    halo = halo_of_edges(from_left, from_right)
    is_right = iota((ROWS, LANES), 1) < LANES // 2
    halo = jnp.where(is_right & (space == lax.axis_size("space") - 1), right, halo)
    return jnp.where(jnp.logical_not(is_right) & (space == 0), left, halo)


def split(state):
    high = state.astype(jnp.bfloat16)
    low = (state - high.astype(jnp.float32)).astype(jnp.bfloat16)
    return jnp.concatenate([high, high, low, high], axis=0)


def lower(added, current):
    return jnp.concatenate([added[:COND], added[COND:] + current], axis=0)


def multiply(weights, state):
    return jnp.dot(weights, split(state), preferred_element_type=jnp.float32)


def step(state, weights, width):
    return shift_once(multiply(weights, state), width)


def shift_once(product, width):
    outs = []
    for b in range(0, product.shape[1], width):
        e = b + width
        out = product[:ROWS, b:e] + pltpu.roll(product[ROWS : 2 * ROWS, b:e], 1, 1)
        outs.append(lower(out, pltpu.roll(product[2 * ROWS :, b:e], width - 1, 1)))
    return outs[0] if len(outs) == 1 else jnp.concatenate(outs, axis=1)


def shift_twice(product, width):
    outs = []
    for b in range(0, product.shape[1], width):
        e = b + width
        out = product[:ROWS, b:e]
        for m, shift in ((1, 1), (2, width - 1), (3, 2)):
            out = out + pltpu.roll(product[m * ROWS : (m + 1) * ROWS, b:e], shift, 1)
        outs.append(lower(out, pltpu.roll(product[4 * ROWS :, b:e], width - 2, 1)))
    return outs[0] if len(outs) == 1 else jnp.concatenate(outs, axis=1)


def tile_of(ref, k):
    return ref[:, k * LANES : (k + 1) * LANES]


def step_tiles(load, store, count, weights, ring, group):
    first = iota((ROWS, LANES), 1) == 0
    last = iota((COND, LANES), 1) == LANES - 1
    here, before, after = {}, {}, {}
    order = [count - 1, *range(count - 1)] if ring else list(range(count))
    for at in range(0, count, group):
        some = order[at : at + group]
        product = multiply(weights, jnp.concatenate([load(k) for k in some], axis=1))
        for j, k in enumerate(some):
            part = product[:, j * LANES : (j + 1) * LANES]
            here[k] = part[:ROWS]
            before[k] = pltpu.roll(part[ROWS : 2 * ROWS], 1, 1)
            after[k] = pltpu.roll(part[2 * ROWS :], LANES - 1, 1)
        for k in list(here):
            left, right = k - 1, k + 1
            if ring:
                left, right = left % count, right % count
            elif k == 0:
                left = k
            elif k == count - 1:
                right = k
            if left in before and right in after:
                tile = here.pop(k) + jnp.where(first, before[left], before[k])
                store(k, lower(tile, jnp.where(last, after[right], after[k])))


def prepare_kernel(fine_ref, coarse_ref, forcing_ref, out_ref, staged_ref, sem):
    copy = pltpu.make_async_copy(forcing_ref, staged_ref, sem)
    copy.start()

    def product(a, b):
        return jnp.dot(
            a, b, precision=lax.Precision.HIGHEST, preferred_element_type=jnp.float32
        )

    def put(at, whole):
        high = whole.astype(jnp.bfloat16)
        rest = whole - high.astype(jnp.float32)
        low = rest.astype(jnp.bfloat16)
        least = (rest - low.astype(jnp.float32)).astype(jnp.bfloat16)
        parts = jnp.concatenate([high, low, high, least], axis=1)
        out_ref[at : at + whole.shape[0], :] = parts

    for m, blocks_ref in enumerate((fine_ref, coarse_ref)):
        p_v, k_v, p_i, k_i = (blocks_ref[r] for r in range(4))
        k_pk = product(k_i, jnp.concatenate([p_v, k_v], axis=1))
        kp, kk = k_pk[:, :COND], k_pk[:, COND:]
        zero = jnp.zeros_like(kk)

        def block(a, b, c, d):
            top = jnp.concatenate([a, b], axis=1)
            return jnp.concatenate([top, jnp.concatenate([c, d], axis=1)], axis=0)

        own = block(p_v, -k_v, kp, p_i - 2.0 * kk)
        before = block(zero, k_v, zero, kk)
        after = block(zero, zero, -kp, kk)
        put(FINE if m == 0 else COARSE, jnp.concatenate([own, before, after[COND:]], axis=0))
        if m == 1:
            square = product(
                jnp.concatenate([own, before, after], axis=0),
                jnp.concatenate([own, before, after], axis=1),
            )

            def pair(a, b):
                return square[a * ROWS : (a + 1) * ROWS, b * ROWS : (b + 1) * ROWS]

            twice = [
                pair(0, 0) + pair(1, 2) + pair(2, 1),
                pair(0, 1) + pair(1, 0),
                pair(0, 2) + pair(2, 0),
                pair(1, 1),
                pair(2, 2)[COND:],
            ]
            put(COARSE_TWICE, jnp.concatenate(twice, axis=0))
    copy.wait()


def prepare(fine_blocks, coarse_blocks, forcing):
    vmem = pl.BlockSpec(memory_space=pltpu.VMEM)
    return pl.pallas_call(
        prepare_kernel,
        out_shape=(
            pltpu.VMEM((OPERATORS, 4 * ROWS), jnp.bfloat16),
            pltpu.VMEM(forcing.shape, jnp.float32),
        ),
        in_specs=[vmem, vmem, pl.BlockSpec(memory_space=pltpu.HBM)],
        out_specs=(vmem, vmem),
        scratch_shapes=[pltpu.SemaphoreType.DMA],
        compiler_params=pltpu.CompilerParams(vmem_limit_bytes=VMEM_LIMIT),
        name="prepare",
    )(fine_blocks, coarse_blocks, pltpu.with_memory_space_constraint(forcing, pltpu.HBM))


def edges_kernel(
    f_first, f_last, c_first, c_last, i_first, i_last, low_ref, high_ref, low_guess_ref, high_guess_ref
):
    count = f_first.shape[0]
    for n in range(count):
        low_ref[n] = pack_edge(f_first[n], 0)
        high_ref[n] = pack_edge(f_last[n], LANES - REACH)
    low_guess_ref[...] = pack_edge(c_first[0], 0)
    high_guess_ref[...] = pack_edge(c_last[0], LANES - REACH)
    low_ref[count] = low_guess_ref[...]
    high_ref[count] = high_guess_ref[...]
    low_ref[count + 1] = pack_edge(i_first[...], 0)
    high_ref[count + 1] = pack_edge(i_last[...], LANES - REACH)


def cut_edges(forcing, c_guess, initial):
    count, _, length = forcing.shape
    end = length // LANES - 1

    def both(shape, at):
        return [pl.BlockSpec(shape, lambda g, a=a: at(a)) for a in (0, end)]

    shape = jax.ShapeDtypeStruct((count + 2, 8, LANES), jnp.float32)
    whole = pl.BlockSpec(shape.shape, lambda g: (0, 0, 0))
    guess = jax.ShapeDtypeStruct((8, LANES), jnp.float32)
    whole_guess = pl.BlockSpec(guess.shape, lambda g: (0, 0))
    return pl.pallas_call(
        edges_kernel,
        grid=(1,),
        out_shape=(shape, shape, guess, guess),
        in_specs=both((count, ROWS, LANES), lambda a: (0, 0, a))
        + both((1, ROWS, LANES), lambda a: (0, 0, a))
        + both((ROWS, LANES), lambda a: (0, a)),
        out_specs=(whole, whole, whole_guess, whole_guess),
        name="edges",
    )(forcing, forcing, c_guess, c_guess, initial, initial)


def write_parts(out_ref, main, halo, at):
    groups = out_ref.shape[0]
    length = main.shape[1]
    part = length // groups
    tiles = part // LANES

    def tile(k):
        if k < 0 or k == length // LANES:
            return halo
        return main[:, k * LANES : (k + 1) * LANES]

    for j in range(groups):
        for i in range(tiles):
            out_ref[j, at + ROWS * i : at + ROWS * (i + 1), :] = tile(j * tiles + i)
        rim = join_halo(tile((j + 1) * tiles), tile(j * tiles - 1))
        out_ref[j, at + ROWS * tiles : at + ROWS * tiles + RIM, :] = pack_edge(rim, LANES - REACH // 2)


def source_halo_kernel(forcing_ref, left_ref, right_ref, halo_ref):
    count, _, length = forcing_ref.shape
    for n in range(count):
        halo_ref[n] = make_halo(
            left_ref[n], right_ref[n], forcing_ref[n, :, :LANES], forcing_ref[n, :, length - LANES :]
        )


def source_halos(forcing, left, right):
    vmem = pl.BlockSpec(memory_space=pltpu.VMEM)
    return pl.pallas_call(
        source_halo_kernel,
        out_shape=pltpu.VMEM((forcing.shape[0], ROWS, LANES), jnp.float32),
        in_specs=[vmem] * 3,
        out_specs=vmem,
        compiler_params=pltpu.CompilerParams(vmem_limit_bytes=VMEM_LIMIT),
        name="source_halos",
    )(forcing, left, right)


def first_kernel(
    forcing_ref,
    source_halo_ref,
    begin_ref,
    initial_ref,
    guess_ref,
    left_ref,
    right_ref,
    begin_left_ref,
    begin_right_ref,
    weights_ref,
    out_ref,
    value_ref,
    even_ref,
    odd_ref,
):
    steps, _, length = forcing_ref.shape
    tiles = length // LANES
    guess_at, initial_at = left_ref.shape[0] - 2, left_ref.shape[0] - 1
    own_ref = guess_ref.at[0]
    is_first = lax.axis_index("tm") == 0

    def begin(k):
        return jnp.where(is_first, tile_of(initial_ref, k), tile_of(begin_ref, k))

    begin_halo = make_halo(
        jnp.where(is_first, left_ref[initial_at], begin_left_ref[...]),
        jnp.where(is_first, right_ref[initial_at], begin_right_ref[...]),
        begin(0),
        begin(tiles - 1),
    )
    states = (even_ref, odd_ref)
    for n in range(steps):

        def load(k, n=n):
            if n > 0:
                return tile_of(states[n % 2], k)
            return begin(k - 1) if 0 < k <= tiles else begin_halo

        def store(k, tile, n=n):
            inside = 0 < k <= tiles
            tile = tile + (tile_of(forcing_ref.at[n], k - 1) if inside else source_halo_ref[n])
            if n == steps - 1 and inside:
                value_ref[:, (k - 1) * LANES : k * LANES] = tile
            else:
                states[(n + 1) % 2][:, k * LANES : (k + 1) * LANES] = tile

        step_tiles(load, store, tiles + 2, weights_ref[FINE:COARSE], False, 3)

    end = states[steps % 2]
    halo = join_halo(tile_of(end, tiles + 1), tile_of(end, 0))
    value_ref[:, length:] = halo
    guess_halo = make_halo(
        left_ref[guess_at], right_ref[guess_at], tile_of(own_ref, 0), tile_of(own_ref, tiles - 1)
    )
    write_parts(out_ref, value_ref[:, :length] - own_ref[...], halo - guess_halo, 0)


def first_chain(
    forcing,
    source_halo,
    begin,
    initial,
    c_guess,
    left,
    right,
    begin_left,
    begin_right,
    weights,
    groups,
):
    steps, _, length = forcing.shape
    rows = length // groups // LANES * ROWS + RIM
    vmem = pl.BlockSpec(memory_space=pltpu.VMEM)
    return pl.pallas_call(
        first_kernel,
        out_shape=(
            pltpu.VMEM((groups, rows, LANES), jnp.float32),
            pltpu.VMEM((ROWS, length + LANES), jnp.float32),
        ),
        in_specs=[vmem, vmem, vmem, vmem, vmem, vmem, vmem, vmem, vmem, vmem],
        out_specs=(vmem, vmem),
        scratch_shapes=[
            pltpu.VMEM((ROWS, length + 2 * LANES), jnp.float32),
            pltpu.VMEM((ROWS, length + 2 * LANES), jnp.float32),
        ],
        compiler_params=pltpu.CompilerParams(vmem_limit_bytes=VMEM_LIMIT),
        cost_estimate=cost(steps, length, forcing.size),
        name="first_chain",
    )(
        forcing,
        source_halo,
        begin,
        initial,
        c_guess,
        left,
        right,
        begin_left,
        begin_right,
        weights,
    )


def cost(steps, columns, elements):
    return pl.CostEstimate(
        flops=steps * columns * 80 * 128 * 16, bytes_accessed=8 * elements, transcendentals=0
    )


def coarse_kernel(parts_ref, weights_ref, out_ref, even_ref, odd_ref):
    groups = parts_ref.shape[0]
    tiles = (parts_ref.shape[1] - RIM) // ROWS
    width = (tiles + 1) * LANES

    states = (even_ref, odd_ref)
    for n in range(8):
        for t in range(groups - 1):

            def load(k, n=n, t=t):
                if n > 0:
                    return tile_of(states[n % 2], t * (tiles + 1) + k)
                if k < tiles:
                    return parts_ref[t, ROWS * k : ROWS * (k + 1), :]
                return unpack_edge(parts_ref[t, ROWS * tiles : ROWS * tiles + RIM, :], LANES - REACH // 2)

            def store(k, tile, n=n, t=t):
                at = t * width + k * LANES
                states[(n + 1) % 2][:, at : at + LANES] = tile

            step_tiles(load, store, tiles + 1, weights_ref[FINE:COARSE], True, tiles + 1)

    def put(t, ring):
        for i in range(tiles):
            out_ref[t, ROWS * i : ROWS * (i + 1), :] = ring[:, i * LANES : (i + 1) * LANES]

    resid = [even_ref[:, t * width : (t + 1) * width] for t in range(groups - 1)]
    second = range(1, groups - 2, 2)
    carried = step(
        jnp.concatenate([resid[t] for t in second], axis=1),
        weights_ref[COARSE:COARSE_TWICE],
        width,
    )
    out_ref[0] = jnp.zeros_like(out_ref[0])
    correction = resid[0]
    put(1, correction)
    for m, t in enumerate(second):
        both = multiply(weights_ref[COARSE:OPERATORS], correction)
        put(t + 1, shift_once(both[:ONCE], width) + resid[t])
        together = carried[:, m * width : (m + 1) * width] + resid[t + 1]
        correction = shift_twice(both[ONCE:], width) + together
        put(t + 2, correction)


def coarse_solve(parts, weights):
    groups, rows, _ = parts.shape
    tiles = (rows - RIM) // ROWS
    return pl.pallas_call(
        coarse_kernel,
        out_shape=pltpu.VMEM((groups, ROWS * tiles, LANES), jnp.float32),
        scratch_shapes=[pltpu.VMEM((ROWS, (groups - 1) * (tiles + 1) * LANES), jnp.float32)] * 2,
        compiler_params=pltpu.CompilerParams(vmem_limit_bytes=VMEM_LIMIT),
        cost_estimate=cost(12, groups * tiles * LANES, parts.size),
        name="coarse_solve",
    )(parts, weights)


def second_kernel(
    forcing_ref,
    source_halo_ref,
    begin_ref,
    initial_ref,
    left_ref,
    right_ref,
    weights_ref,
    out_ref,
    states_ref,
    source_ref,
    low_ref,
    high_ref,
    source_sems,
    out_sems,
):
    steps = states_ref.shape[0]
    length = forcing_ref.shape[2]
    tiles = length // LANES
    initial_at = left_ref.shape[0] - 1
    is_first = lax.axis_index("tm") == 0

    def source(n):
        return pltpu.make_async_copy(forcing_ref.at[n], source_ref.at[n], source_sems.at[n])

    def result(n):
        return pltpu.make_async_copy(states_ref.at[n], out_ref.at[n], out_sems.at[n])

    for n in range(AHEAD):
        source(n).start()

    def begin(k):
        return jnp.where(is_first, tile_of(initial_ref, k), tile_of(begin_ref, k))

    begin_halo = jnp.where(
        is_first,
        make_halo(left_ref[initial_at], right_ref[initial_at], begin(0), begin(tiles - 1)),
        tile_of(begin_ref, tiles),
    )
    for n in range(steps):
        source(n).wait()
        if n + AHEAD < steps:
            source(n + AHEAD).start()

        def load(k, n=n):
            if 0 < k <= tiles:
                return tile_of(states_ref.at[n - 1], k - 1) if n > 0 else begin(k - 1)
            if n == 0:
                return begin_halo
            return low_ref[n - 1] if k == 0 else high_ref[n - 1]

        def store(k, tile, n=n):
            if 0 < k <= tiles:
                states_ref[n, :, (k - 1) * LANES : k * LANES] = tile + tile_of(source_ref.at[n], k - 1)
            elif k == 0:
                low_ref[n] = tile + source_halo_ref[n]
            else:
                high_ref[n] = tile + source_halo_ref[n]

        step_tiles(load, store, tiles + 2, weights_ref[FINE:COARSE], False, 3)
        result(n).start()
    for n in range(steps):
        result(n).wait()


def second_chain(forcing, source_halo, begin, initial, left, right, weights):
    count, _, length = forcing.shape
    steps = count - 1
    hbm = pl.BlockSpec(memory_space=pltpu.HBM)
    vmem = pl.BlockSpec(memory_space=pltpu.VMEM)
    return pl.pallas_call(
        second_kernel,
        out_shape=jax.ShapeDtypeStruct(forcing.shape, jnp.float32),
        in_specs=[hbm, vmem, vmem, vmem, vmem, vmem, vmem],
        out_specs=hbm,
        scratch_shapes=[
            pltpu.VMEM((steps, ROWS, length), jnp.float32),
            pltpu.VMEM((steps, ROWS, length), jnp.float32),
            pltpu.VMEM((steps, ROWS, LANES), jnp.float32),
            pltpu.VMEM((steps, ROWS, LANES), jnp.float32),
            pltpu.SemaphoreType.DMA((steps,)),
            pltpu.SemaphoreType.DMA((steps,)),
        ],
        compiler_params=pltpu.CompilerParams(vmem_limit_bytes=VMEM_LIMIT),
        cost_estimate=cost(count, length, 2 * forcing.size),
        name="second_chain",
    )(
        pltpu.with_memory_space_constraint(forcing, pltpu.HBM),
        source_halo,
        begin,
        initial,
        left,
        right,
        weights,
    )


def correct_kernel(value_ref, parts_ref, states_ref, out_ref):
    del states_ref
    groups = parts_ref.shape[0]
    tiles = out_ref.shape[2] // groups // LANES
    for j in range(groups):
        for i in range(tiles):
            at = (j * tiles + i) * LANES
            out_ref[0, :, at : at + LANES] = (
                value_ref[:, at : at + LANES] + parts_ref[j, ROWS * i : ROWS * (i + 1), :]
            )


def correct_last(value, parts, states):
    count, _, length = states.shape
    return pl.pallas_call(
        correct_kernel,
        grid=(1,),
        out_shape=jax.ShapeDtypeStruct(states.shape, jnp.float32),
        in_specs=[
            pl.BlockSpec(value.shape, lambda g: (0, 0)),
            pl.BlockSpec(parts.shape, lambda g: (0, 0, 0)),
            pl.BlockSpec(memory_space=pl.ANY),
        ],
        out_specs=pl.BlockSpec((1, ROWS, length), lambda g: (count - 1, 0, 0)),
        input_output_aliases={2: 0},
        compiler_params=pltpu.CompilerParams(vmem_limit_bytes=VMEM_LIMIT),
        name="correct_last",
    )(value, parts, states)


def body(initial, c_guess, forcing, fine_blocks, coarse_blocks):
    groups = lax.axis_size("tm")
    spaces = lax.axis_size("space")
    up = [(i, (i + 1) % spaces) for i in range(spaces)]
    down = [(b, a) for a, b in up]
    to_next = [(i, (i + 1) % groups) for i in range(groups)]

    def to_next_and(pairs):
        return [(t * spaces + a, u * spaces + b) for t, u in to_next for a, b in pairs]

    begin = lax.ppermute(c_guess[0], "tm", to_next)
    low, high, low_guess, high_guess = cut_edges(forcing, c_guess, initial)
    right = lax.ppermute(low, "space", down)
    left = lax.ppermute(high, "space", up)
    begin_right = lax.ppermute(low_guess, ("tm", "space"), to_next_and(down))
    begin_left = lax.ppermute(high_guess, ("tm", "space"), to_next_and(up))
    weights, staged = prepare(fine_blocks, coarse_blocks, forcing)
    source_halo = source_halos(staged, left, right)
    parts, value = first_chain(
        staged,
        source_halo,
        begin,
        initial,
        c_guess,
        left,
        right,
        begin_left,
        begin_right,
        weights,
        groups,
    )
    parts = lax.all_to_all(parts, "tm", 0, 0, tiled=True)
    begin = lax.ppermute(value, "tm", to_next[:-1])
    parts = coarse_solve(parts, weights)
    parts = lax.all_to_all(parts, "tm", 0, 0, tiled=True)
    states = second_chain(forcing, source_halo, begin, initial, left, right, weights)
    return correct_last(value, parts, states)


def solution(mesh):
    in_specs = (P(None, "space"), P("tm", None, "space"), P("tm", None, "space"), P(), P())
    out_specs = P("tm", None, "space")
    return jax.shard_map(body, mesh=mesh, in_specs=in_specs, out_specs=out_specs, check_vma=False)
```
